32 devices in a mesh: groups: 2 (over y), block: 16 (over z, x, core).
Axes of the slice: x: 2, y: 2, z: 4, core: 2. Of those that a mesh axis runs over, the one named last changes fastest.
Arguments:
- queries: bfloat16 [49152, 1024], P(('groups', 'block')), parts along dimension 0, may hold values from -6 to 6
- keys: bfloat16 [49152, 1024], P(('groups', 'block')), parts along dimension 0, may hold values from -16 to 16
- values: bfloat16 [49152, 1024], P(('groups', 'block')), parts along dimension 0, may hold values from -12 to 12
Outputs:
- attended: bfloat16 [49152, 1024], P(('groups', 'block')), parts along dimension 0
The draws below stay inside these ranges and needn't reach their ends.
There are 2 independent parts, one for each index of `groups`. The reference program is written for one: setup_inputs(seed, part) draws one part's arguments, and reference() takes and returns one part's arrays. A program takes and returns all parts, laid end to end along the dimension named above; each array names one. Nothing has to cross between parts.
All inputs are finite; a program needn't handle non-finite values.
Results may differ from the reference program's by a relative error of at most 0.0029.
Values sent between devices are 32-bit elements; how exact they have to be, the bound alone decides.
A program may use at most 128 MiB of HBM per device.

```python
import jax
import jax.numpy as jnp
from jax import lax

HEADS = 8
HEAD_DIM = 128
SPAN = 128
TOKENS = 24576
HD = 1024


def one_order(key):
    return jax.random.permutation(key, HEAD_DIM)


def shared_offsets(key):
    count = TOKENS // SPAN
    offset_key, order_key = jax.random.split(jax.random.fold_in(key, 5))
    offsets = 3.0 * jax.random.normal(offset_key, (count, 1, HEADS, HEAD_DIM), jnp.float32)
    orders = jax.vmap(one_order)(jax.random.split(order_key, HEADS))
    paired = jnp.take_along_axis(offsets, orders[None, None], axis=-1)
    return (offsets, paired)


def draw_keys(key, part):
    count = TOKENS // SPAN
    base_key, scale_key = jax.random.split(jax.random.fold_in(key, 11))
    base = jax.random.normal(base_key, (count, SPAN, HEADS, HEAD_DIM), jnp.float32)
    scales = jnp.exp(jax.random.uniform(scale_key, (count, 1, HEADS, 1), jnp.float32, -1.2, 1.2))
    offsets, paired = shared_offsets(key)
    keys = (base * scales + offsets).reshape(TOKENS, HEADS * HEAD_DIM)
    return jnp.clip(keys, -16.0, 16.0).astype(jnp.bfloat16)


def draw_values(key, part):
    count = TOKENS // SPAN
    base_key, shift_key = jax.random.split(jax.random.fold_in(key, 23))
    base = jax.random.normal(base_key, (count, SPAN, HEADS, HEAD_DIM), jnp.float32)
    shifts = jax.random.normal(shift_key, (count, 1, HEADS, HEAD_DIM), jnp.float32)
    offsets, paired = shared_offsets(key)
    values = (base + shifts + 0.5 * paired).reshape(TOKENS, HEADS * HEAD_DIM)
    return jnp.clip(values, -12.0, 12.0).astype(jnp.bfloat16)


def block_levels(rng, dims, pieces, low, top_value):
    level = 1.0
    for axis_at, blocks in pieces:
        heights = jax.random.uniform(jax.random.fold_in(jax.random.fold_in(rng, 6), axis_at), (blocks,), jnp.float32, low / len(pieces), top_value / len(pieces))
        level = level * jnp.repeat(jnp.exp(heights), dims[axis_at] // blocks).reshape((-1,) + (1,) * (len(dims) - 1 - axis_at))
    return level


def scatter_about(stream_key, extent, width, reach, cuts=(), kind=jnp.bfloat16):
    entries = jax.random.normal(stream_key, extent, jnp.float32) * width
    if len(cuts) > 0:
        entries = block_levels(stream_key, extent, cuts, -0.22, 0.18) * entries
    return jnp.clip(entries, min=-reach, max=reach).astype(kind)


def setup_inputs(seed: int = 0, part: int = 0) -> dict:
    splits = jax.random.split(jax.random.key(seed), 4)
    own_keys = jax.random.split(jax.random.fold_in(splits[3], part), 4)
    return {
        "queries": scatter_about(own_keys[0], (TOKENS, HD), 1.0, 6.0, ((0, 16),)),
        "keys": draw_keys(jax.random.fold_in(jax.random.fold_in(splits[3], part), 71), part),
        "values": draw_values(jax.random.fold_in(jax.random.fold_in(splits[3], part), 71), part),
    }


def features(x):
    return lax.optimization_barrier((jax.nn.elu(x.astype(jnp.float32)) + 1.0).astype(jnp.bfloat16)).astype(jnp.float32)


def reference(queries, keys, values):
    count = TOKENS // SPAN
    fq = features(queries).reshape(count, SPAN, HEADS, HEAD_DIM)
    fk = features(keys).reshape(count, SPAN, HEADS, HEAD_DIM)
    vv = values.astype(jnp.float32).reshape(count, SPAN, HEADS, HEAD_DIM)
    causal = jnp.arange(SPAN)[:, None] >= jnp.arange(SPAN)[None, :]

    def step(carry, inputs):
        state, norm = carry
        qc, kc, vc = inputs
        state_b = lax.optimization_barrier(state.astype(jnp.bfloat16)).astype(jnp.float32)
        inter = jnp.einsum('chd,hde->che', qc, state_b)
        den_inter = jnp.einsum('chd,hd->ch', qc, norm)
        scores = jnp.einsum('chd,khd->hck', qc, kc)
        scores = jnp.where(causal[None], scores, jnp.float32(0.0))
        scores_b = lax.optimization_barrier(scores.astype(jnp.bfloat16)).astype(jnp.float32)
        intra = jnp.einsum('hck,khe->che', scores_b, vc)
        den = den_inter + jnp.transpose(jnp.sum(scores, axis=-1), (1, 0))
        out = ((inter + intra) / den[..., None]).astype(jnp.bfloat16)
        state = state + jnp.einsum('chd,che->hde', kc, vc)
        norm = norm + jnp.sum(kc, axis=0)
        return (state, norm), out

    start = (jnp.zeros((HEADS, HEAD_DIM, HEAD_DIM), jnp.float32), jnp.zeros((HEADS, HEAD_DIM), jnp.float32))
    final, outs = lax.scan(step, start, (fq, fk, vv))
    return outs.reshape(TOKENS, HEADS * HEAD_DIM)
```

```python
import functools

import jax
import jax.numpy as jnp
from jax import lax
from jax.experimental import pallas as pl
from jax.experimental.pallas import tpu as pltpu
from jax.sharding import PartitionSpec as P

HEADS = 8
DIM = 128
TILE = 256
HALF = TILE // 2
F32 = jnp.float32
BF16 = jnp.bfloat16


def features(x):
    x = x.astype(F32)
    return jnp.where(x > 0.0, x + 1.0, jnp.exp(x)).astype(BF16)


def nt(a, b):
    return lax.dot_general(a, b, (((1,), (1,)), ((), ())), preferred_element_type=F32)


def tn(a, b):
    return lax.dot_general(a, b, (((0,), (0,)), ((), ())), preferred_element_type=F32)


def nn(a, b):
    return jnp.dot(a, b, preferred_element_type=F32)


def kernel(
    n, q_hbm, k_hbm, v_hbm, o_hbm, qb, kb, vb, ob, num, den, kvt, ksum,
    give, got, back, before, in_sem, out_sem, s1, r1, s2, r2,
):
    rows = qb.shape[1]
    tiles = rows // TILE
    piece = HEADS * DIM // n
    per_head = n // HEADS
    me = lax.axis_index("block")

    def cols(h):
        return pl.ds(pl.multiple_of(h * DIM, DIM), DIM)

    def load(which, src, dst, h):
        return pltpu.make_async_copy(src.at[:, cols(h)], dst.at[h], in_sem.at[which, h])

    def send_total(o, slot):
        return pltpu.make_async_remote_copy(
            src_ref=give.at[o], dst_ref=got.at[slot], send_sem=s1.at[o],
            recv_sem=r1.at[slot], device_id={"block": o},
        )

    def send_back(o, slot):
        return pltpu.make_async_remote_copy(
            src_ref=back.at[o], dst_ref=before.at[slot], send_sem=s2.at[o],
            recv_sem=r2.at[slot], device_id={"block": o},
        )

    def store(h):
        return pltpu.make_async_copy(ob.at[h], o_hbm.at[:, cols(h)], out_sem.at[h])

    for h in range(HEADS):
        load(0, k_hbm, kb, h).start()
        load(1, v_hbm, vb, h).start()
    for h in range(HEADS):
        load(2, q_hbm, qb, h).start()

    barrier = pltpu.get_barrier_semaphore()

    @pl.loop(0, n)
    def _(o):
        @pl.when(o != me)
        def _():
            pl.semaphore_signal(barrier, inc=1, device_id={"block": o})

    def state(h):
        load(0, k_hbm, kb, h).wait()
        load(1, v_hbm, vb, h).wait()
        total = jnp.zeros((DIM, DIM), F32)
        norm = jnp.zeros((8, DIM), F32)
        for t in range(tiles):
            at = pl.ds(t * TILE, TILE)
            fk = features(kb[h, at, :])
            kb[h, at, :] = fk
            kvt[h, t] = total
            ksum[h, t] = norm
            total = total + tn(vb[h, at, :], fk)
            part = jnp.sum(fk.astype(F32).reshape(TILE // 8, 8, DIM), axis=0)
            norm = norm + jnp.broadcast_to(jnp.sum(part, axis=0, keepdims=True), (8, DIM))
        return total, norm

    def share(h, total, norm):
        for j in range(per_head):
            o = h * per_head + j
            give[o, pl.ds(0, piece), :] = total[j * piece : (j + 1) * piece]
            give[o, pl.ds(piece, 8), :] = norm

            @pl.when(o != me)
            def _():
                send_total(o, me).start()

            @pl.when(o == me)
            def _():
                got[me] = give[o]

    total, norm = state(0)
    pl.semaphore_wait(barrier, n - 1)
    share(0, total, norm)

    @pl.loop(1, HEADS)
    def _(h):
        share(h, *state(h))

    later = lax.broadcasted_iota(jnp.int32, (HALF, HALF), 1) > lax.broadcasted_iota(
        jnp.int32, (HALF, HALF), 0
    )
    ones = jnp.ones((TILE, DIM), BF16)

    def local(h):
        load(2, q_hbm, qb, h).wait()
        for t in range(tiles):
            at = pl.ds(t * TILE, TILE)
            fq = features(qb[h, at, :])
            qb[h, at, :] = fq
            fk = kb[h, at, :]
            vo = jnp.concatenate([vb[h, at, :], ones], axis=1)
            top = jnp.where(later, 0.0, nt(fq[:HALF], fk[:HALF])).astype(BF16)
            low = nt(fq[HALF:], fk)
            low = jnp.concatenate(
                [low[:, :HALF].astype(BF16), jnp.where(later, 0.0, low[:, HALF:]).astype(BF16)],
                axis=1,
            )
            r = jnp.concatenate([nn(top, vo[:HALF]), nn(low, vo)], axis=0)
            if t:
                w = jnp.concatenate(
                    [kvt[h, t], jnp.broadcast_to(ksum[h, t][:1], (DIM, DIM))], axis=0
                ).astype(BF16)
                r = r + nt(fq, w)
            num[h, at, :] = r[:, :DIM]
            den[h, at, :] = r[:, DIM:]

    def answer():
        def step(src, acc):
            @pl.when(src != me)
            def _():
                send_total(src, src).wait_recv()

            back[src] = acc

            @pl.when(src != me)
            def _():
                send_back(src, me).start()

            @pl.when(src == me)
            def _():
                before[me] = acc

            return acc + got[src]

        lax.fori_loop(0, n, step, jnp.zeros((piece + 8, DIM), F32))

    split = HEADS // 2

    @pl.loop(0, split)
    def _(h):
        local(h)

    answer()

    @pl.loop(split, HEADS)
    def _(h):
        local(h)

    @pl.loop(0, HEADS)
    def _(h):
        parts = []
        for j in range(per_head):
            o = h * per_head + j

            @pl.when(o != me)
            def _():
                send_back(o, o).wait_recv()

            parts.append(before[o, pl.ds(0, piece), :])
        norm = before[h * per_head, pl.ds(piece, 8), :]
        w = jnp.concatenate(
            parts + [jnp.broadcast_to(norm[:1], (DIM, DIM))], axis=0
        ).astype(BF16)
        for t in range(tiles):
            at = pl.ds(t * TILE, TILE)
            r = nt(qb[h, at, :], w)
            d = den[h, at, :] + r[:, DIM:]
            x = pl.reciprocal(d, approx=True)
            x = x * (2.0 - d * x)
            ob[h, at, :] = ((num[h, at, :] + r[:, :DIM]) * x).astype(BF16)
        store(h).start()

    @pl.loop(0, n)
    def _(o):
        @pl.when(o != me)
        def _():
            send_total(o, me).wait_send()
            send_back(o, me).wait_send()

    @pl.loop(0, HEADS)
    def _(h):
        store(h).wait()


def solution(mesh):
    n = mesh.shape["block"]
    piece = HEADS * DIM // n

    def per_device(q, k, v):
        rows = q.shape[0]
        tiles = rows // TILE
        whole = pltpu.VMEM((HEADS, rows, DIM), BF16)
        wide = pltpu.VMEM((HEADS, rows, DIM), F32)
        slots = pltpu.VMEM((n, piece + 8, DIM), F32)
        line = pltpu.SemaphoreType.DMA((n,))
        return pl.pallas_call(
            functools.partial(kernel, n),
            out_shape=jax.ShapeDtypeStruct(q.shape, BF16),
            in_specs=[pl.BlockSpec(memory_space=pl.ANY)] * 3,
            out_specs=pl.BlockSpec(memory_space=pl.ANY),
            scratch_shapes=[
                whole, whole, whole, whole, wide, wide,
                pltpu.VMEM((HEADS, tiles, DIM, DIM), F32),
                pltpu.VMEM((HEADS, tiles, 8, DIM), F32),
                slots, slots, slots, slots,
                pltpu.SemaphoreType.DMA((3, HEADS)),
                pltpu.SemaphoreType.DMA((HEADS,)),
                line, line, line, line,
            ],
            compiler_params=pltpu.CompilerParams(
                collective_id=0, has_side_effects=True, vmem_limit_bytes=50 * 2**20
            ),
        )(q, k, v)

    spec = P(("groups", "block"), None)
    return jax.shard_map(
        per_device, mesh=mesh, in_specs=(spec,) * 3, out_specs=spec, check_vma=False
    )
```

```python
import functools

import jax
import jax.numpy as jnp
from jax import lax
from jax.experimental import pallas as pl
from jax.experimental.pallas import tpu as pltpu
from jax.sharding import PartitionSpec as P

HEADS = 8
DIM = 128
TILE = 256
HALF = TILE // 2
F32 = jnp.float32
BF16 = jnp.bfloat16


def features(x):
    x = x.astype(F32)
    return jnp.where(x > 0.0, x + 1.0, jnp.exp(x)).astype(BF16)


def nt(a, b):
    return lax.dot_general(a, b, (((1,), (1,)), ((), ())), preferred_element_type=F32)


def tn(a, b):
    return lax.dot_general(a, b, (((0,), (0,)), ((), ())), preferred_element_type=F32)


def nn(a, b):
    return jnp.dot(a, b, preferred_element_type=F32)


def kernel(
    n, q_hbm, k_hbm, v_hbm, o_hbm, qb, kb, vb, ob, num, den, kvt, ksum,
    mine, theirs, cin, cout, xin, xout, pin, pout,
    in_sem, out_sem, t_send, t_recv, z_send, z_recv, x_send, x_recv, p_send, p_recv,
):
    rows = qb.shape[1]
    tiles = rows // TILE
    half = HEADS // 2
    levels = n // 4
    me = lax.axis_index("block")
    core = lax.rem(me, 2)
    side = lax.rem(me // 2, 2)
    level = me // 4
    twin = me + 1 - 2 * core
    across = me + 2 - 4 * side

    def cols(h):
        return pl.ds(pl.multiple_of(h * DIM, DIM), DIM)

    def load(which, src, dst, h):
        return pltpu.make_async_copy(src.at[:, cols(h)], dst.at[h], in_sem.at[which, h])

    def remote(src, dst, send, recv, i, to):
        return pltpu.make_async_remote_copy(
            src_ref=src.at[i], dst_ref=dst.at[i], send_sem=send.at[i], recv_sem=recv.at[i],
            device_id={"block": to},
        )

    def to_twin(h):
        return remote(mine, theirs, t_send, t_recv, h, twin)

    def up(i):
        return remote(cout, cin, z_send, z_recv, i, me + 4)

    def over(i):
        return remote(xout, xin, x_send, x_recv, i, across)

    def prefix(i):
        return remote(pout, pin, p_send, p_recv, i, twin)

    def store(h):
        return pltpu.make_async_copy(ob.at[h], o_hbm.at[:, cols(h)], out_sem.at[h])

    for i in range(half):
        for h in (i, i + half):
            load(0, k_hbm, kb, h).start()
            load(1, v_hbm, vb, h).start()
    for h in range(HEADS):
        load(2, q_hbm, qb, h).start()

    barrier = pltpu.get_barrier_semaphore()
    pl.semaphore_signal(barrier, inc=1, device_id={"block": twin})
    pl.semaphore_signal(barrier, inc=1, device_id={"block": across})

    @pl.when(level > 0)
    def _():
        pl.semaphore_signal(barrier, inc=1, device_id={"block": me - 4})

    @pl.when(level < levels - 1)
    def _():
        pl.semaphore_signal(barrier, inc=1, device_id={"block": me + 4})

    @pl.when(level == 0)
    def _():
        cin[...] = jnp.zeros(cin.shape, F32)

    def state(h):
        load(0, k_hbm, kb, h).wait()
        load(1, v_hbm, vb, h).wait()
        total = jnp.zeros((DIM, DIM), F32)
        norm = jnp.zeros((8, DIM), F32)
        for t in range(tiles):
            at = pl.ds(t * TILE, TILE)
            fk = features(kb[h, at, :])
            kb[h, at, :] = fk
            if t:
                kvt[h, t] = total
                ksum[h, t] = norm
            total = total + tn(vb[h, at, :], fk)
            part = jnp.sum(fk.astype(F32).reshape(TILE // 8, 8, DIM), axis=0)
            norm = norm + jnp.broadcast_to(jnp.sum(part, axis=0, keepdims=True), (8, DIM))
        mine[h, pl.ds(0, DIM), :] = total
        mine[h, pl.ds(DIM, 8), :] = norm

    def share(i):
        to_twin(i).start()

        @pl.when(core == 0)
        def _():
            to_twin(i + half).start()

    later = lax.broadcasted_iota(jnp.int32, (HALF, HALF), 1) > lax.broadcasted_iota(
        jnp.int32, (HALF, HALF), 0
    )
    ones = jnp.ones((TILE, DIM), BF16)

    def local(h):
        load(2, q_hbm, qb, h).wait()
        for t in range(tiles):
            at = pl.ds(t * TILE, TILE)
            fq = features(qb[h, at, :])
            qb[h, at, :] = fq
            fk = kb[h, at, :]
            vo = jnp.concatenate([vb[h, at, :], ones], axis=1)
            top = jnp.where(later, 0.0, nt(fq[:HALF], fk[:HALF])).astype(BF16)
            low = nt(fq[HALF:], fk)
            low = jnp.concatenate(
                [low[:, :HALF].astype(BF16), jnp.where(later, 0.0, low[:, HALF:]).astype(BF16)],
                axis=1,
            )
            r = jnp.concatenate([nn(top, vo[:HALF]), nn(low, vo)], axis=0)
            if t:
                w = jnp.concatenate(
                    [kvt[h, t], jnp.broadcast_to(ksum[h, t][:1], (DIM, DIM))], axis=0
                ).astype(BF16)
                r = r + nt(fq, w)
            num[h, at, :] = r[:, :DIM]
            den[h, at, :] = r[:, DIM:]

    def climb(i):
        h = core * half + i
        to_twin(h).wait_recv()

        @pl.when(level > 0)
        def _():
            up(i).wait_recv()

        below = cin[i]
        both = below + (mine[h] + theirs[h])

        @pl.when(level < levels - 1)
        def _():
            cout[i] = both
            up(i).start()

        @pl.when(side == 0)
        def _():
            xout[i] = both

        @pl.when(side == 1)
        def _():
            xout[i] = below

        over(i).start()

    def cross(i):
        over(i).wait_recv()
        pout[i] = cin[i] + xin[i]
        prefix(i).start()

    def steps(u):
        i = u - 1 - 2 * level

        @pl.when((i >= 0) & (i < half))
        def _():
            climb(i)

        j = u - 3 - 2 * level

        @pl.when((j >= 0) & (j < half))
        def _():
            cross(j)

    def finish(h, before):
        w = jnp.concatenate(
            [before[:DIM], jnp.broadcast_to(before[DIM : DIM + 1], (DIM, DIM))], axis=0
        ).astype(BF16)
        for t in range(tiles):
            at = pl.ds(t * TILE, TILE)
            r = nt(qb[h, at, :], w)
            d = den[h, at, :] + r[:, DIM:]
            x = pl.reciprocal(d, approx=True)
            x = x * (2.0 - d * x)
            ob[h, at, :] = ((num[h, at, :] + r[:, :DIM]) * x).astype(BF16)
        store(h).start()

    state(0)
    state(half)
    near = 2 + jnp.where(level > 0, 1, 0) + jnp.where(level < levels - 1, 1, 0)
    pl.semaphore_wait(barrier, near)
    share(0)

    @pl.loop(1, half)
    def _(u):
        state(u)
        state(u + half)
        share(u)
        steps(u)

    @pl.loop(half, half + HEADS)
    def _(u):
        local(u - half)
        steps(u)

    @pl.loop(half + HEADS, max(half + HEADS, 2 * levels + 1 + half))
    def _(u):
        steps(u)

    @pl.loop(0, half)
    def _(i):
        h = core * half + i

        prefix(i).wait_send()

        @pl.when(core == 1)
        def _():
            pout[i] = pout[i] + theirs[h]

        finish(h, pout[i])

    @pl.loop(0, half)
    def _(i):
        h = (1 - core) * half + i
        prefix(i).wait_recv()

        @pl.when(core == 1)
        def _():
            to_twin(h).wait_recv()
            pin[i] = pin[i] + theirs[h]

        finish(h, pin[i])

    @pl.loop(0, half)
    def _(i):
        to_twin(i).wait_send()

        @pl.when(core == 0)
        def _():
            to_twin(i + half).wait_send()

        @pl.when(level < levels - 1)
        def _():
            up(i).wait_send()

        over(i).wait_send()

    @pl.loop(0, HEADS)
    def _(h):
        store(h).wait()


def solution(mesh):
    n = mesh.shape["block"]

    def per_device(q, k, v):
        rows = q.shape[0]
        tiles = rows // TILE
        whole = pltpu.VMEM((HEADS, rows, DIM), BF16)
        wide = pltpu.VMEM((HEADS, rows, DIM), F32)
        totals = pltpu.VMEM((HEADS, DIM + 8, DIM), F32)
        parts = pltpu.VMEM((HEADS // 2, DIM + 8, DIM), F32)
        line = pltpu.SemaphoreType.DMA((HEADS // 2,))
        full = pltpu.SemaphoreType.DMA((HEADS,))
        return pl.pallas_call(
            functools.partial(kernel, n),
            out_shape=jax.ShapeDtypeStruct(q.shape, BF16),
            in_specs=[pl.BlockSpec(memory_space=pl.ANY)] * 3,
            out_specs=pl.BlockSpec(memory_space=pl.ANY),
            scratch_shapes=[
                whole, whole, whole, whole, wide, wide,
                pltpu.VMEM((HEADS, tiles, DIM, DIM), F32),
                pltpu.VMEM((HEADS, tiles, 8, DIM), F32),
                totals, totals, parts, parts, parts, parts, parts, parts,
                pltpu.SemaphoreType.DMA((3, HEADS)),
                full, full, full,
                line, line, line, line, line, line,
            ],
            compiler_params=pltpu.CompilerParams(
                collective_id=0, has_side_effects=True, vmem_limit_bytes=50 * 2**20
            ),
        )(q, k, v)

    spec = P(("groups", "block"), None)
    return jax.shard_map(
        per_device, mesh=mesh, in_specs=(spec,) * 3, out_specs=spec, check_vma=False
    )
```

```python
import functools

import jax
import jax.numpy as jnp
from jax import lax
from jax.experimental import pallas as pl
from jax.experimental.pallas import tpu as pltpu
from jax.sharding import PartitionSpec as P

HEADS = 8
DIM = 128
TILE = 256
HALF = TILE // 2
F32 = jnp.float32
BF16 = jnp.bfloat16


def features(x):
    x = x.astype(F32)
    return jnp.where(x > 0.0, x + 1.0, jnp.exp(x)).astype(BF16)


def nt(a, b):
    return lax.dot_general(a, b, (((1,), (1,)), ((), ())), preferred_element_type=F32)


def tn(a, b):
    return lax.dot_general(a, b, (((0,), (0,)), ((), ())), preferred_element_type=F32)


def nn(a, b):
    return jnp.dot(a, b, preferred_element_type=F32)


def kernel(
    n, q_hbm, k_hbm, v_hbm, o_hbm, qb, kb, vb, ob, fq, fk, num, den, prior,
    mine, theirs, cin, cout, xin, xout, pin, pout,
    in_sem, out_sem, t_send, t_recv, z_send, z_recv, x_send, x_recv, p_send, p_recv,
):
    rows = qb.shape[1]
    tiles = rows // TILE
    half = HEADS // 2
    levels = n // 4
    me = lax.axis_index("block")
    core = lax.rem(me, 2)
    side = lax.rem(me // 2, 2)
    level = me // 4
    twin = me + 1 - 2 * core
    across = me + 2 - 4 * side

    def cols(h):
        return pl.ds(pl.multiple_of(h * DIM, DIM), DIM)

    def load(which, src, dst, h):
        return pltpu.make_async_copy(src.at[:, cols(h)], dst.at[h], in_sem.at[which, h])

    def remote(src, dst, send, recv, i, to):
        return pltpu.make_async_remote_copy(
            src_ref=src.at[i], dst_ref=dst.at[i], send_sem=send.at[i], recv_sem=recv.at[i],
            device_id={"block": to},
        )

    def to_twin(h):
        return remote(mine, theirs, t_send, t_recv, h, twin)

    def up(i):
        return remote(cout, cin, z_send, z_recv, i, me + 4)

    def over(i):
        return remote(xout, xin, x_send, x_recv, i, across)

    def prefix(i):
        return remote(pout, pin, p_send, p_recv, i, twin)

    def store(h):
        return pltpu.make_async_copy(ob.at[h], o_hbm.at[:, cols(h)], out_sem.at[h])

    for i in range(half):
        for h in (i, i + half):
            load(0, k_hbm, kb, h).start()
            load(1, v_hbm, vb, h).start()
    for h in range(HEADS):
        load(2, q_hbm, qb, h).start()

    barrier = pltpu.get_barrier_semaphore()
    pl.semaphore_signal(barrier, inc=1, device_id={"block": twin})
    pl.semaphore_signal(barrier, inc=1, device_id={"block": across})

    @pl.when(level > 0)
    def _():
        pl.semaphore_signal(barrier, inc=1, device_id={"block": me - 4})

    @pl.when(level < levels - 1)
    def _():
        pl.semaphore_signal(barrier, inc=1, device_id={"block": me + 4})

    @pl.when(level == 0)
    def _():
        cin[...] = jnp.zeros(cin.shape, F32)

    ones = jnp.ones((TILE, DIM), BF16)

    def arrive(*heads):
        for h in heads:
            load(0, k_hbm, kb, h).wait()
            load(1, v_hbm, vb, h).wait()

    def state(h):
        total = None
        for t in range(tiles):
            at = pl.ds(t * TILE, TILE)
            f = features(kb[h, at, :])
            fk[h, at, :] = f
            add = tn(f, jnp.concatenate([vb[h, at, :], ones], axis=1))
            if t:
                prior[h, t] = total.astype(BF16)
            total = total + add if t else add
        mine[h, pl.ds(0, DIM), :] = total[:, :DIM]
        mine[h, pl.ds(DIM, 8), :] = total[:, DIM:].T[:8]

    def share(i):
        to_twin(i).start()

        @pl.when(core == 0)
        def _():
            to_twin(i + half).start()

    later = lax.broadcasted_iota(jnp.int32, (HALF, HALF), 1) > lax.broadcasted_iota(
        jnp.int32, (HALF, HALF), 0
    )
    none = jnp.zeros((HALF, HALF), BF16)

    def local(h):
        for t in range(tiles):
            at = pl.ds(t * TILE, TILE)
            f = features(qb[h, at, :])
            fq[h, at, :] = f
            sc = nt(f, fk[h, at, :])
            top = jnp.where(later, 0.0, sc[:HALF, :HALF]).astype(BF16)
            low = jnp.where(later, 0.0, sc[HALF:, HALF:]).astype(BF16)
            left = jnp.concatenate([top, sc[HALF:, :HALF].astype(BF16)], axis=0)
            right = jnp.concatenate([none, low], axis=0)
            a = jnp.concatenate([left, right], axis=1)
            b = jnp.concatenate([vb[h, at, :], ones], axis=1)
            if t:
                a = jnp.concatenate([a, f], axis=1)
                b = jnp.concatenate([b, prior[h, t]], axis=0)
            r = nn(a, b)
            num[h, at, :] = r[:, :DIM]
            den[h, at, :] = r[:, DIM:]

    def climb(i):
        h = core * half + i
        to_twin(h).wait_recv()

        @pl.when(level > 0)
        def _():
            up(i).wait_recv()

        below = cin[i]
        both = below + (mine[h] + theirs[h])

        @pl.when(level < levels - 1)
        def _():
            cout[i] = both
            up(i).start()

        @pl.when(side == 0)
        def _():
            xout[i] = both

        @pl.when(side == 1)
        def _():
            xout[i] = below

        over(i).start()

    def cross(i):
        over(i).wait_recv()
        pout[i] = cin[i] + xin[i]
        prefix(i).start()

    def steps(u):
        i = u - 1 - 2 * level

        @pl.when((i >= 0) & (i < half))
        def _():
            climb(i)

        j = u - 3 - 2 * level

        @pl.when((j >= 0) & (j < half))
        def _():
            cross(j)

    def finish(h, before):
        norm = jnp.broadcast_to(before[DIM : DIM + 1], (DIM, DIM)).T
        w = jnp.concatenate([before[:DIM], norm], axis=1).astype(BF16)
        for t in range(tiles):
            at = pl.ds(t * TILE, TILE)
            r = nn(fq[h, at, :], w)
            d = den[h, at, :] + r[:, DIM:]
            x = pl.reciprocal(d, approx=True)
            x = x * (2.0 - d * x)
            ob[h, at, :] = ((num[h, at, :] + r[:, :DIM]) * x).astype(BF16)

    arrive(0, half)
    state(0)
    state(half)
    near = 2 + jnp.where(level > 0, 1, 0) + jnp.where(level < levels - 1, 1, 0)
    pl.semaphore_wait(barrier, near)
    share(0)

    @pl.loop(1, half)
    def _(u):
        arrive(u, u + half)
        state(u)
        state(u + half)
        share(u)
        steps(u)

    @pl.loop(0, half)
    def _(u):
        load(2, q_hbm, qb, 2 * u).wait()
        load(2, q_hbm, qb, 2 * u + 1).wait()
        local(2 * u)
        local(2 * u + 1)
        steps(half + 2 * u)
        steps(half + 2 * u + 1)

    @pl.loop(half + HEADS, max(half + HEADS, 2 * levels + 1 + half))
    def _(u):
        steps(u)

    @pl.loop(0, half)
    def _(i):
        own = core * half + i
        other = (1 - core) * half + i
        prefix(i).wait()

        @pl.when(core == 1)
        def _():
            to_twin(other).wait_recv()
            pout[i] = pout[i] + theirs[own]
            pin[i] = pin[i] + theirs[other]

        finish(own, pout[i])
        finish(other, pin[i])
        store(own).start()
        store(other).start()

    @pl.loop(0, half)
    def _(i):
        to_twin(i).wait_send()

        @pl.when(core == 0)
        def _():
            to_twin(i + half).wait_send()

        @pl.when(level < levels - 1)
        def _():
            up(i).wait_send()

        over(i).wait_send()

    @pl.loop(0, HEADS)
    def _(h):
        store(h).wait()


def solution(mesh):
    n = mesh.shape["block"]

    def per_device(q, k, v):
        rows = q.shape[0]
        tiles = rows // TILE
        whole = pltpu.VMEM((HEADS, rows, DIM), BF16)
        wide = pltpu.VMEM((HEADS, rows, DIM), F32)
        totals = pltpu.VMEM((HEADS, DIM + 8, DIM), F32)
        parts = pltpu.VMEM((HEADS // 2, DIM + 8, DIM), F32)
        line = pltpu.SemaphoreType.DMA((HEADS // 2,))
        full = pltpu.SemaphoreType.DMA((HEADS,))
        return pl.pallas_call(
            functools.partial(kernel, n),
            out_shape=jax.ShapeDtypeStruct(q.shape, BF16),
            in_specs=[pl.BlockSpec(memory_space=pl.ANY)] * 3,
            out_specs=pl.BlockSpec(memory_space=pl.ANY),
            scratch_shapes=[
                whole, whole, whole, whole, whole, whole, wide, wide,
                pltpu.VMEM((HEADS, tiles, DIM, 2 * DIM), BF16),
                totals, totals, parts, parts, parts, parts, parts, parts,
                pltpu.SemaphoreType.DMA((3, HEADS)),
                full, full, full,
                line, line, line, line, line, line,
            ],
            compiler_params=pltpu.CompilerParams(
                collective_id=0, has_side_effects=True, vmem_limit_bytes=50 * 2**20
            ),
        )(q, k, v)

    spec = P(("groups", "block"), None)
    return jax.shard_map(
        per_device, mesh=mesh, in_specs=(spec,) * 3, out_specs=spec, check_vma=False
    )
```

```python
import functools

import jax
import jax.numpy as jnp
from jax import lax
from jax.experimental import pallas as pl
from jax.experimental.pallas import tpu as pltpu
from jax.sharding import PartitionSpec as P

HEADS = 8
DIM = 128
TILE = 128
F32 = jnp.float32
BF16 = jnp.bfloat16


def features(x):
    x = x.astype(F32)
    return jnp.where(x > 0.0, x + 1.0, jnp.exp(x)).astype(BF16)


def nt(a, b):
    return lax.dot_general(a, b, (((1,), (1,)), ((), ())), preferred_element_type=F32)


def tn(a, b):
    return lax.dot_general(a, b, (((0,), (0,)), ((), ())), preferred_element_type=F32)


def nn(a, b):
    return jnp.dot(a, b, preferred_element_type=F32)


def kernel(
    n, q_hbm, k_hbm, v_hbm, o_hbm, qb, kb, vb, ob, fq, fk, scores, prior,
    mine, theirs, cin, cout, xin, xout, pin, pout,
    in_sem, out_sem, t_send, t_recv, z_send, z_recv, x_send, x_recv, p_send, p_recv,
):
    rows = qb.shape[1]
    tiles = rows // TILE
    half = HEADS // 2
    levels = n // 4
    me = lax.axis_index("block")
    core = lax.rem(me, 2)
    side = lax.rem(me // 2, 2)
    level = me // 4
    twin = me + 1 - 2 * core
    across = me + 2 - 4 * side

    def cols(h):
        return pl.ds(pl.multiple_of(h * DIM, DIM), DIM)

    def load(which, src, dst, h):
        return pltpu.make_async_copy(src.at[:, cols(h)], dst.at[h], in_sem.at[which, h])

    def remote(src, dst, send, recv, i, to):
        return pltpu.make_async_remote_copy(
            src_ref=src.at[i], dst_ref=dst.at[i], send_sem=send.at[i], recv_sem=recv.at[i],
            device_id={"block": to},
        )

    def to_twin(h):
        return remote(mine, theirs, t_send, t_recv, h, twin)

    def up(i):
        return remote(cout, cin, z_send, z_recv, i, me + 4)

    def over(i):
        return remote(xout, xin, x_send, x_recv, i, across)

    def prefix(i):
        return remote(pout, pin, p_send, p_recv, i, twin)

    def store(h):
        return pltpu.make_async_copy(ob.at[h], o_hbm.at[:, cols(h)], out_sem.at[h])

    for i in range(half):
        for h in (i, i + half):
            load(0, k_hbm, kb, h).start()
            load(1, v_hbm, vb, h).start()
    for h in range(HEADS):
        load(2, q_hbm, qb, h).start()

    barrier = pltpu.get_barrier_semaphore()
    pl.semaphore_signal(barrier, inc=1, device_id={"block": twin})
    pl.semaphore_signal(barrier, inc=1, device_id={"block": across})

    @pl.when(level > 0)
    def _():
        pl.semaphore_signal(barrier, inc=1, device_id={"block": me - 4})

    @pl.when(level < levels - 1)
    def _():
        pl.semaphore_signal(barrier, inc=1, device_id={"block": me + 4})

    @pl.when(level == 0)
    def _():
        cin[...] = jnp.zeros(cin.shape, F32)

    ones = jnp.ones((TILE, DIM), BF16)

    def arrive(*heads):
        for h in heads:
            load(0, k_hbm, kb, h).wait()
            load(1, v_hbm, vb, h).wait()

    def state(h):
        total = None
        for t in range(tiles):
            at = pl.ds(t * TILE, TILE)
            f = features(kb[h, at, :])
            fk[h, at, :] = f
            add = tn(f, jnp.concatenate([vb[h, at, :], ones], axis=1))
            if t:
                prior[h, t] = total
            total = total + add if t else add
        mine[h, pl.ds(0, DIM), :] = total[:, :DIM]
        mine[h, pl.ds(DIM, 8), :] = total[:, DIM:].T[:8]

    def share(i):
        to_twin(i).start()

        @pl.when(core == 0)
        def _():
            to_twin(i + half).start()

    later = lax.broadcasted_iota(jnp.int32, (TILE, TILE), 1) > lax.broadcasted_iota(
        jnp.int32, (TILE, TILE), 0
    )

    def local(h):
        for t in range(tiles):
            at = pl.ds(t * TILE, TILE)
            f = features(qb[h, at, :])
            fq[h, at, :] = f
            sc = nt(f, fk[h, at, :])
            scores[h, at, :] = jnp.where(later, 0.0, sc).astype(BF16)

    def climb(i):
        h = core * half + i
        to_twin(h).wait_recv()

        @pl.when(level > 0)
        def _():
            up(i).wait_recv()

        below = cin[i]
        both = below + (mine[h] + theirs[h])

        @pl.when(level < levels - 1)
        def _():
            cout[i] = both
            up(i).start()

        @pl.when(side == 0)
        def _():
            xout[i] = both

        @pl.when(side == 1)
        def _():
            xout[i] = below

        over(i).start()

    def cross(i):
        over(i).wait_recv()
        pout[i] = cin[i] + xin[i]
        prefix(i).start()

    def steps(u):
        i = u - 1 - 2 * level

        @pl.when((i >= 0) & (i < half))
        def _():
            climb(i)

        j = u - 3 - 2 * level

        @pl.when((j >= 0) & (j < half))
        def _():
            cross(j)

    def finish(h, before):
        norm = jnp.broadcast_to(before[DIM : DIM + 1], (DIM, DIM)).T
        start = jnp.concatenate([before[:DIM], norm], axis=1)
        for t in range(tiles):
            at = pl.ds(t * TILE, TILE)
            w = (start + prior[h, t] if t else start).astype(BF16)
            a = jnp.concatenate([scores[h, at, :], fq[h, at, :]], axis=1)
            b = jnp.concatenate([vb[h, at, :], ones], axis=1)
            r = nn(a, jnp.concatenate([b, w], axis=0))
            d = r[:, DIM:]
            x = pl.reciprocal(d, approx=True)
            x = x * (2.0 - d * x)
            ob[h, at, :] = (r[:, :DIM] * x).astype(BF16)

    def close(i):
        own = core * half + i
        other = (1 - core) * half + i
        prefix(i).wait()

        @pl.when(core == 1)
        def _():
            to_twin(other).wait_recv()
            pout[i] = pout[i] + theirs[own]
            pin[i] = pin[i] + theirs[other]

        finish(own, pout[i])
        finish(other, pin[i])
        store(own).start()
        store(other).start()

    arrive(0, half)
    state(0)
    state(half)
    near = 2 + jnp.where(level > 0, 1, 0) + jnp.where(level < levels - 1, 1, 0)
    pl.semaphore_wait(barrier, near)
    share(0)

    @pl.loop(1, half)
    def _(u):
        arrive(u, u + half)
        state(u)
        state(u + half)
        share(u)
        steps(u)

    @pl.loop(0, half)
    def _(u):
        load(2, q_hbm, qb, 2 * u).wait()
        load(2, q_hbm, qb, 2 * u + 1).wait()
        local(2 * u)
        local(2 * u + 1)
        steps(half + u)

    first = lax.max(2 * half, half + 2 * level)

    @pl.loop(2 * half, max(2 * half, half + 2 * (levels - 1)) + half)
    def _(u):
        steps(u)
        i = u - first

        @pl.when((i >= 0) & (i < half))
        def _():
            close(i)

    @pl.loop(0, half)
    def _(i):
        to_twin(i).wait_send()

        @pl.when(core == 0)
        def _():
            to_twin(i + half).wait_send()

        @pl.when(level < levels - 1)
        def _():
            up(i).wait_send()

        over(i).wait_send()

    @pl.loop(0, HEADS)
    def _(h):
        store(h).wait()


def solution(mesh):
    n = mesh.shape["block"]

    def per_device(q, k, v):
        rows = q.shape[0]
        tiles = rows // TILE
        whole = pltpu.VMEM((HEADS, rows, DIM), BF16)
        totals = pltpu.VMEM((HEADS, DIM + 8, DIM), F32)
        parts = pltpu.VMEM((HEADS // 2, DIM + 8, DIM), F32)
        line = pltpu.SemaphoreType.DMA((HEADS // 2,))
        full = pltpu.SemaphoreType.DMA((HEADS,))
        return pl.pallas_call(
            functools.partial(kernel, n),
            out_shape=jax.ShapeDtypeStruct(q.shape, BF16),
            in_specs=[pl.BlockSpec(memory_space=pl.ANY)] * 3,
            out_specs=pl.BlockSpec(memory_space=pl.ANY),
            scratch_shapes=[
                whole, whole, whole, whole, whole, whole, whole,
                pltpu.VMEM((HEADS, tiles, DIM, 2 * DIM), F32),
                totals, totals, parts, parts, parts, parts, parts, parts,
                pltpu.SemaphoreType.DMA((3, HEADS)),
                full, full, full,
                line, line, line, line, line, line,
            ],
            compiler_params=pltpu.CompilerParams(
                collective_id=0, has_side_effects=True, vmem_limit_bytes=50 * 2**20
            ),
        )(q, k, v)

    spec = P(("groups", "block"), None)
    return jax.shard_map(
        per_device, mesh=mesh, in_specs=(spec,) * 3, out_specs=spec, check_vma=False
    )
```

```python
import functools

import jax
import jax.numpy as jnp
from jax import lax
from jax.experimental import pallas as pl
from jax.experimental.pallas import tpu as pltpu
from jax.sharding import PartitionSpec as P

HEADS = 8
DIM = 128
TILE = 128
WIDE = 256
CUT = DIM // 2
CHUNKS = ((0, CUT + 8), (CUT + 8, CUT))
F32 = jnp.float32
BF16 = jnp.bfloat16


def features(x):
    x = x.astype(F32)
    return jnp.where(x > 0.0, x + 1.0, jnp.exp(x)).astype(BF16)


def nt(a, b):
    return lax.dot_general(a, b, (((1,), (1,)), ((), ())), preferred_element_type=F32)


def tn(a, b):
    return lax.dot_general(a, b, (((0,), (0,)), ((), ())), preferred_element_type=F32)


def nn(a, b):
    return jnp.dot(a, b, preferred_element_type=F32)


def kernel(
    n, q_hbm, k_hbm, v_hbm, o_hbm, qb, kb, vb, ob, fq, fk, scores, prior,
    mine, theirs, cin, cout, xin, xout, pin, pout,
    in_sem, out_sem, t_send, t_recv, z_send, z_recv, x_send, x_recv, p_send, p_recv,
):
    rows = qb.shape[1]
    tiles = rows // TILE
    half = HEADS // 2
    levels = n // 4
    me = lax.axis_index("block")
    core = lax.rem(me, 2)
    side = lax.rem(me // 2, 2)
    level = me // 4
    twin = me + 1 - 2 * core
    across = me + 2 - 4 * side

    def cols(h):
        return pl.ds(pl.multiple_of(h * DIM, DIM), DIM)

    def load(which, src, dst, h):
        return pltpu.make_async_copy(src.at[:, cols(h)], dst.at[h], in_sem.at[which, h])

    def remote(src, dst, send, recv, i, p, to):
        at = pl.ds(*CHUNKS[p])
        return pltpu.make_async_remote_copy(
            src_ref=src.at[i, at], dst_ref=dst.at[i, at], send_sem=send.at[i, p],
            recv_sem=recv.at[i, p], device_id={"block": to},
        )

    def to_twin(h, p):
        return remote(mine, theirs, t_send, t_recv, h, p, twin)

    def up(i, p):
        return remote(cout, cin, z_send, z_recv, i, p, me + 4)

    def over(i, p):
        return remote(xout, xin, x_send, x_recv, i, p, across)

    def prefix(i, p):
        return remote(pout, pin, p_send, p_recv, i, p, twin)

    def store(h):
        return pltpu.make_async_copy(ob.at[h], o_hbm.at[:, cols(h)], out_sem.at[h])

    for i in range(half):
        for h in (i, i + half):
            load(0, k_hbm, kb, h).start()
            load(1, v_hbm, vb, h).start()
    for h in range(HEADS):
        load(2, q_hbm, qb, h).start()

    barrier = pltpu.get_barrier_semaphore()
    pl.semaphore_signal(barrier, inc=1, device_id={"block": twin})
    pl.semaphore_signal(barrier, inc=1, device_id={"block": across})

    @pl.when(level > 0)
    def _():
        pl.semaphore_signal(barrier, inc=1, device_id={"block": me - 4})

    @pl.when(level < levels - 1)
    def _():
        pl.semaphore_signal(barrier, inc=1, device_id={"block": me + 4})

    @pl.when(level == 0)
    def _():
        cin[...] = jnp.zeros(cin.shape, F32)

    def arrive(*heads):
        for h in heads:
            load(0, k_hbm, kb, h).wait()
            load(1, v_hbm, vb, h).wait()

    def state(h):
        ones = jnp.ones((WIDE, DIM), BF16)
        total = None
        for t in range(rows // WIDE):
            at = pl.ds(t * WIDE, WIDE)
            f = features(kb[h, at, :])
            fk[h, at, :] = f
            add = tn(f, jnp.concatenate([vb[h, at, :], ones], axis=1))
            total = total + add if t else add
        mine[h, pl.ds(0, CUT), :] = total[:CUT, :DIM]
        mine[h, pl.ds(CUT, 8), :] = total[:, DIM:].T[:8]
        mine[h, pl.ds(CUT + 8, CUT), :] = total[CUT:, :DIM]

    def share(i):
        for p in range(2):
            to_twin(i, p).start()

        @pl.when(core == 0)
        def _():
            for p in range(2):
                to_twin(i + half, p).start()

    ones = jnp.ones((TILE, DIM), BF16)
    later = lax.broadcasted_iota(jnp.int32, (TILE, TILE), 1) > lax.broadcasted_iota(
        jnp.int32, (TILE, TILE), 0
    )

    def local(h):
        total = None
        for t in range(tiles):
            at = pl.ds(t * TILE, TILE)
            f = features(qb[h, at, :])
            fq[h, at, :] = f
            sc = nt(f, fk[h, at, :])
            scores[h, at, :] = jnp.where(later, 0.0, sc).astype(BF16)
            if t < tiles - 1:
                add = tn(fk[h, at, :], jnp.concatenate([vb[h, at, :], ones], axis=1))
                total = total + add if t else add
                prior[h, t + 1] = total

    def climb(i):
        h = core * half + i
        for p in range(2):
            at = pl.ds(*CHUNKS[p])
            to_twin(h, p).wait_recv()

            @pl.when(level > 0)
            def _():
                up(i, p).wait_recv()

            below = cin[i, at]
            both = below + (mine[h, at] + theirs[h, at])

            @pl.when(level < levels - 1)
            def _():
                cout[i, at] = both
                up(i, p).start()

            @pl.when(side == 0)
            def _():
                xout[i, at] = both

            @pl.when(side == 1)
            def _():
                xout[i, at] = below

            over(i, p).start()

    def cross(i):
        for p in range(2):
            at = pl.ds(*CHUNKS[p])
            over(i, p).wait_recv()
            pout[i, at] = cin[i, at] + xin[i, at]
            prefix(i, p).start()

    def at_turn(t, step):
        @pl.when((t >= 0) & (t < 2 * half) & (lax.rem(t, 2) == 0))
        def _():
            step(lax.div(t, 2))

    def steps(u):
        @pl.when(level > 0)
        def _():
            at_turn(u - 3 - 2 * level, climb)

        at_turn(u - 5 - 2 * level, cross)

    def finish(h, before):
        norm = jnp.broadcast_to(before[CUT : CUT + 1], (DIM, DIM)).T
        state = jnp.concatenate([before[:CUT], before[CUT + 8 :]], axis=0)
        start = jnp.concatenate([state, norm], axis=1)
        for t in range(tiles):
            at = pl.ds(t * TILE, TILE)
            w = (start + prior[h, t] if t else start).astype(BF16)
            a = jnp.concatenate([scores[h, at, :], fq[h, at, :]], axis=1)
            b = jnp.concatenate([vb[h, at, :], ones], axis=1)
            r = nn(a, jnp.concatenate([b, w], axis=0))
            d = r[:, DIM:]
            x = pl.reciprocal(d, approx=True)
            x = x * (2.0 - d * x)
            ob[h, at, :] = (r[:, :DIM] * x).astype(BF16)

    def close(i):
        own = core * half + i
        other = (1 - core) * half + i
        for p in range(2):
            prefix(i, p).wait()

        @pl.when(core == 1)
        def _():
            for p in range(2):
                to_twin(other, p).wait_recv()
            pout[i] = pout[i] + theirs[own]
            pin[i] = pin[i] + theirs[other]

        finish(own, pout[i])
        finish(other, pin[i])
        store(own).start()
        store(other).start()

    arrive(0, half)
    state(0)
    state(half)
    near = 2 + jnp.where(level > 0, 1, 0) + jnp.where(level < levels - 1, 1, 0)
    pl.semaphore_wait(barrier, near)
    share(0)

    @pl.loop(1, half)
    def _(u):
        arrive(u, u + half)
        state(u)
        state(u + half)
        share(u)

        @pl.when(level == 0)
        def _():
            climb(u - 1)

    @pl.when(level == 0)
    def _():
        climb(half - 1)

    tail = half + HEADS

    @pl.loop(half, tail)
    def _(u):
        load(2, q_hbm, qb, u - half).wait()
        local(u - half)
        steps(u)

    first = lax.max(tail, 7 + 2 * level)

    @pl.loop(tail, max(tail, 5 + 2 * levels) + 2 * half)
    def _(u):
        steps(u)
        at_turn(u - first, close)

    @pl.loop(0, half)
    def _(i):
        for p in range(2):
            to_twin(i, p).wait_send()

            @pl.when(core == 0)
            def _():
                to_twin(i + half, p).wait_send()

            @pl.when(level < levels - 1)
            def _():
                up(i, p).wait_send()

            over(i, p).wait_send()

    @pl.loop(0, HEADS)
    def _(h):
        store(h).wait()


def solution(mesh):
    n = mesh.shape["block"]

    def per_device(q, k, v):
        rows = q.shape[0]
        tiles = rows // TILE
        whole = pltpu.VMEM((HEADS, rows, DIM), BF16)
        totals = pltpu.VMEM((HEADS, DIM + 8, DIM), F32)
        parts = pltpu.VMEM((HEADS // 2, DIM + 8, DIM), F32)
        line = pltpu.SemaphoreType.DMA((HEADS // 2, 2))
        full = pltpu.SemaphoreType.DMA((HEADS, 2))
        return pl.pallas_call(
            functools.partial(kernel, n),
            out_shape=jax.ShapeDtypeStruct(q.shape, BF16),
            in_specs=[pl.BlockSpec(memory_space=pl.ANY)] * 3,
            out_specs=pl.BlockSpec(memory_space=pl.ANY),
            scratch_shapes=[
                whole, whole, whole, whole, whole, whole, whole,
                pltpu.VMEM((HEADS, tiles, DIM, 2 * DIM), F32),
                totals, totals, parts, parts, parts, parts, parts, parts,
                pltpu.SemaphoreType.DMA((3, HEADS)),
                pltpu.SemaphoreType.DMA((HEADS,)),
                full, full,
                line, line, line, line, line, line,
            ],
            compiler_params=pltpu.CompilerParams(
                collective_id=0, has_side_effects=True, vmem_limit_bytes=50 * 2**20
            ),
        )(q, k, v)

    spec = P(("groups", "block"), None)
    return jax.shard_map(
        per_device, mesh=mesh, in_specs=(spec,) * 3, out_specs=spec, check_vma=False
    )
```

```python
import functools

import jax
import jax.numpy as jnp
from jax import lax
from jax.experimental import pallas as pl
from jax.experimental.pallas import tpu as pltpu
from jax.sharding import PartitionSpec as P

HEADS = 8
DIM = 128
TILE = 128
WIDE = 256
CUT = DIM // 2
CHUNKS = ((0, CUT + 8), (CUT + 8, CUT))
F32 = jnp.float32
BF16 = jnp.bfloat16


def features(x):
    x = x.astype(F32)
    return jnp.where(x > 0.0, x + 1.0, jnp.exp(x)).astype(BF16)


def nt(a, b):
    return lax.dot_general(a, b, (((1,), (1,)), ((), ())), preferred_element_type=F32)


def tn(a, b):
    return lax.dot_general(a, b, (((0,), (0,)), ((), ())), preferred_element_type=F32)


def nn(a, b):
    return jnp.dot(a, b, preferred_element_type=F32)


def kernel(
    n, q_hbm, k_hbm, v_hbm, o_hbm, qb, kb, vb, ob, fq, fk, scores, prior,
    mine, theirs, cin, cout, xin, xout, pin, pout, home,
    in_sem, out_sem, t_send, t_recv, z_send, z_recv, x_send, x_recv, p_send, p_recv,
):
    rows = qb.shape[1]
    tiles = rows // TILE
    half = HEADS // 2
    levels = n // 4
    me = lax.axis_index("block")
    core = lax.rem(me, 2)
    side = lax.rem(me // 2, 2)
    level = me // 4
    twin = me + 1 - 2 * core
    across = me + 2 - 4 * side

    def cols(h):
        return pl.ds(pl.multiple_of(h * DIM, DIM), DIM)

    def load(which, src, dst, h):
        return pltpu.make_async_copy(src.at[:, cols(h)], dst.at[h], in_sem.at[which, h])

    def remote(src, dst, send, recv, i, p, to):
        at = pl.ds(*CHUNKS[p])
        return pltpu.make_async_remote_copy(
            src_ref=src.at[i, at], dst_ref=dst.at[i, at], send_sem=send.at[i, p],
            recv_sem=recv.at[i, p], device_id={"block": to},
        )

    def to_twin(h, p):
        return remote(mine, theirs, t_send, t_recv, h, p, twin)

    def up(i, p):
        return remote(cout, cin, z_send, z_recv, i, p, me + 4)

    def over(i, p):
        return remote(xout, xin, x_send, x_recv, i, p, across)

    def prefix(i, p):
        return remote(pout, pin, p_send, p_recv, i, p, twin)

    def store(h):
        return pltpu.make_async_copy(ob.at[h], o_hbm.at[:, cols(h)], out_sem.at[h])

    def fetch(i):
        for h in (i, i + half):
            load(0, k_hbm, kb, h).start()
            load(1, v_hbm, vb, h).start()

    fetch(0)
    fetch(1)

    barrier = pltpu.get_barrier_semaphore()
    pl.semaphore_signal(barrier, inc=1, device_id={"block": twin})
    pl.semaphore_signal(barrier, inc=1, device_id={"block": across})

    @pl.when(level > 0)
    def _():
        pl.semaphore_signal(barrier, inc=1, device_id={"block": me - 4})

    @pl.when(level < levels - 1)
    def _():
        pl.semaphore_signal(barrier, inc=1, device_id={"block": me + 4})

    @pl.when(level == 0)
    def _():
        cin[...] = jnp.zeros(cin.shape, F32)

    def arrive(*heads):
        for h in heads:
            load(0, k_hbm, kb, h).wait()
            load(1, v_hbm, vb, h).wait()

    def state(h):
        ones = jnp.ones((WIDE, DIM), BF16)
        total = None
        for t in range(rows // WIDE):
            at = pl.ds(t * WIDE, WIDE)
            f = features(kb[h, at, :])
            fk[h, at, :] = f
            add = tn(f, jnp.concatenate([vb[h, at, :], ones], axis=1))
            total = total + add if t else add
        mine[h, pl.ds(0, CUT), :] = total[:CUT, :DIM]
        mine[h, pl.ds(CUT, 8), :] = total[:, DIM:].T[:8]
        mine[h, pl.ds(CUT + 8, CUT), :] = total[CUT:, :DIM]

    def share(i):
        for p in range(2):
            to_twin((1 - core) * half + i, p).start()

    ones = jnp.ones((TILE, DIM), BF16)
    later = lax.broadcasted_iota(jnp.int32, (TILE, TILE), 1) > lax.broadcasted_iota(
        jnp.int32, (TILE, TILE), 0
    )

    def local(h):
        total = None
        for t in range(tiles):
            at = pl.ds(t * TILE, TILE)
            f = features(qb[h, at, :])
            fq[h, at, :] = f
            sc = nt(f, fk[h, at, :])
            scores[h, at, :] = jnp.where(later, 0.0, sc).astype(BF16)
            if t < tiles - 1:
                add = tn(fk[h, at, :], jnp.concatenate([vb[h, at, :], ones], axis=1))
                total = total + add if t else add
                prior[h, t + 1] = total

    def climb(i):
        h = core * half + i
        for p in range(2):
            at = pl.ds(*CHUNKS[p])
            to_twin(h, p).wait_recv()

            @pl.when(level > 0)
            def _():
                up(i, p).wait_recv()

            below = cin[i, at]
            both = below + (mine[h, at] + theirs[h, at])

            @pl.when(level < levels - 1)
            def _():
                cout[i, at] = both
                up(i, p).start()

            @pl.when(side == 0)
            def _():
                xout[i, at] = both

            @pl.when(side == 1)
            def _():
                xout[i, at] = below

            over(i, p).start()

    def cross(i):
        for p in range(2):
            at = pl.ds(*CHUNKS[p])
            over(i, p).wait_recv()
            chip = cin[i, at] + xin[i, at]

            @pl.when(core == 0)
            def _():
                home[i, at] = chip
                pout[i, at] = chip + mine[i, at]

            @pl.when(core == 1)
            def _():
                home[i, at] = chip + theirs[i + half, at]
                pout[i, at] = chip

            prefix(i, p).start()

    def at_turn(t, step):
        @pl.when((t >= 0) & (t < 2 * half) & (lax.rem(t, 2) == 0))
        def _():
            step(lax.div(t, 2))

    def steps(u):
        @pl.when(level > 0)
        def _():
            at_turn(u - 3 - 2 * level, climb)

        at_turn(u - 5 - 2 * level, cross)

    def finish(h, before):
        norm = jnp.broadcast_to(before[CUT : CUT + 1], (DIM, DIM)).T
        state = jnp.concatenate([before[:CUT], before[CUT + 8 :]], axis=0)
        start = jnp.concatenate([state, norm], axis=1)
        for t in range(tiles):
            at = pl.ds(t * TILE, TILE)
            w = (start + prior[h, t] if t else start).astype(BF16)
            a = jnp.concatenate([scores[h, at, :], fq[h, at, :]], axis=1)
            b = jnp.concatenate([vb[h, at, :], ones], axis=1)
            r = nn(a, jnp.concatenate([b, w], axis=0))
            d = r[:, DIM:]
            x = pl.reciprocal(d, approx=True)
            x = x * (2.0 - d * x)
            ob[h, at, :] = (r[:, :DIM] * x).astype(BF16)

    def close(i):
        own = core * half + i
        other = (1 - core) * half + i
        finish(own, home[i])
        store(own).start()
        for p in range(2):
            prefix(i, p).wait()
        finish(other, pin[i])
        store(other).start()

    arrive(0, half)
    fetch(2)
    state(0)
    state(half)
    near = 2 + jnp.where(level > 0, 1, 0) + jnp.where(level < levels - 1, 1, 0)
    pl.semaphore_wait(barrier, near)
    share(0)

    @pl.loop(1, half)
    def _(u):
        arrive(u, u + half)

        @pl.when(u == 1)
        def _():
            fetch(3)

        @pl.when(u > 1)
        def _():
            for j in range(half):
                load(2, q_hbm, qb, (u - 2) * half + j).start()

        state(u)
        state(u + half)
        share(u)

        @pl.when(level == 0)
        def _():
            climb(u - 1)

    @pl.when(level == 0)
    def _():
        climb(half - 1)

    tail = half + HEADS

    @pl.loop(half, tail)
    def _(u):
        load(2, q_hbm, qb, u - half).wait()
        local(u - half)
        steps(u)

    first = lax.max(tail, 7 + 2 * level)

    @pl.loop(tail, max(tail, 5 + 2 * levels) + 2 * half)
    def _(u):
        steps(u)
        at_turn(u - first, close)

    @pl.loop(0, half)
    def _(i):
        for p in range(2):
            to_twin((1 - core) * half + i, p).wait_send()

            @pl.when(level < levels - 1)
            def _():
                up(i, p).wait_send()

            over(i, p).wait_send()

    @pl.loop(0, HEADS)
    def _(h):
        store(h).wait()


def solution(mesh):
    n = mesh.shape["block"]

    def per_device(q, k, v):
        rows = q.shape[0]
        tiles = rows // TILE
        whole = pltpu.VMEM((HEADS, rows, DIM), BF16)
        totals = pltpu.VMEM((HEADS, DIM + 8, DIM), F32)
        parts = pltpu.VMEM((HEADS // 2, DIM + 8, DIM), F32)
        line = pltpu.SemaphoreType.DMA((HEADS // 2, 2))
        full = pltpu.SemaphoreType.DMA((HEADS, 2))
        return pl.pallas_call(
            functools.partial(kernel, n),
            out_shape=jax.ShapeDtypeStruct(q.shape, BF16),
            in_specs=[pl.BlockSpec(memory_space=pl.ANY)] * 3,
            out_specs=pl.BlockSpec(memory_space=pl.ANY),
            scratch_shapes=[
                whole, whole, whole, whole, whole, whole, whole,
                pltpu.VMEM((HEADS, tiles, DIM, 2 * DIM), F32),
                totals, totals, parts, parts, parts, parts, parts, parts, parts,
                pltpu.SemaphoreType.DMA((3, HEADS)),
                pltpu.SemaphoreType.DMA((HEADS,)),
                full, full,
                line, line, line, line, line, line,
            ],
            compiler_params=pltpu.CompilerParams(
                collective_id=0, has_side_effects=True, vmem_limit_bytes=50 * 2**20
            ),
        )(q, k, v)

    spec = P(("groups", "block"), None)
    return jax.shard_map(
        per_device, mesh=mesh, in_specs=(spec,) * 3, out_specs=spec, check_vma=False
    )
```

```python
import functools

import jax
import jax.numpy as jnp
from jax import lax
from jax.experimental import pallas as pl
from jax.experimental.pallas import tpu as pltpu
from jax.sharding import PartitionSpec as P

HEADS = 8
DIM = 128
TILE = 128
WIDE = 256
CUT = DIM // 2
CHUNKS = ((0, CUT + 8), (CUT + 8, CUT))
F32 = jnp.float32
BF16 = jnp.bfloat16


def features(x):
    x = x.astype(F32)
    return jnp.where(x > 0.0, x + 1.0, jnp.exp(x)).astype(BF16)


def nt(a, b):
    return lax.dot_general(a, b, (((1,), (1,)), ((), ())), preferred_element_type=F32)


def tn(a, b):
    return lax.dot_general(a, b, (((0,), (0,)), ((), ())), preferred_element_type=F32)


def nn(a, b):
    return jnp.dot(a, b, preferred_element_type=F32)


def kernel(
    n, q_hbm, k_hbm, v_hbm, o_hbm, qb, kb, vb, ob, fq, fk, scores, prior,
    mine, theirs, cin, cout, xin, xout, pin, pout, home,
    in_sem, out_sem, t_send, t_recv, z_send, z_recv, x_send, x_recv, p_send, p_recv,
):
    rows = qb.shape[1]
    tiles = rows // TILE
    half = HEADS // 2
    levels = n // 4
    me = lax.axis_index("block")
    core = lax.rem(me, 2)
    side = lax.rem(me // 2, 2)
    level = me // 4
    twin = me + 1 - 2 * core
    across = me + 2 - 4 * side

    def cols(h):
        return pl.ds(pl.multiple_of(h * DIM, DIM), DIM)

    def load(which, src, dst, h):
        return pltpu.make_async_copy(src.at[:, cols(h)], dst.at[h], in_sem.at[which, h])

    def remote(src, dst, send, recv, i, p, to):
        at = pl.ds(*CHUNKS[p])
        return pltpu.make_async_remote_copy(
            src_ref=src.at[i, at], dst_ref=dst.at[i, at], send_sem=send.at[i, p],
            recv_sem=recv.at[i, p], device_id={"block": to},
        )

    def to_twin(h, p):
        return remote(mine, theirs, t_send, t_recv, h, p, twin)

    def up(i, p):
        return remote(cout, cin, z_send, z_recv, i, p, me + 4)

    def over(i, p):
        return remote(xout, xin, x_send, x_recv, i, p, across)

    def prefix(i, p):
        return remote(pout, pin, p_send, p_recv, i, p, twin)

    def store(h):
        return pltpu.make_async_copy(ob.at[h], o_hbm.at[:, cols(h)], out_sem.at[h])

    def fetch(i):
        for h in (i, i + half):
            load(0, k_hbm, kb, h).start()
            load(1, v_hbm, vb, h).start()

    fetch(0)
    fetch(1)

    barrier = pltpu.get_barrier_semaphore()
    pl.semaphore_signal(barrier, inc=1, device_id={"block": twin})
    pl.semaphore_signal(barrier, inc=1, device_id={"block": across})

    @pl.when(level > 0)
    def _():
        pl.semaphore_signal(barrier, inc=1, device_id={"block": me - 4})

    @pl.when(level < levels - 1)
    def _():
        pl.semaphore_signal(barrier, inc=1, device_id={"block": me + 4})

    @pl.when(level == 0)
    def _():
        cin[...] = jnp.zeros(cin.shape, F32)

    def arrive(*heads):
        for h in heads:
            load(0, k_hbm, kb, h).wait()
            load(1, v_hbm, vb, h).wait()

    def state(h):
        ones = jnp.ones((WIDE, DIM), BF16)
        total = None
        for t in range(rows // WIDE):
            at = pl.ds(t * WIDE, WIDE)
            f = features(kb[h, at, :])
            fk[h, at, :] = f
            add = tn(f, jnp.concatenate([vb[h, at, :], ones], axis=1))
            total = total + add if t else add
        mine[h, pl.ds(0, CUT), :] = total[:CUT, :DIM]
        mine[h, pl.ds(CUT, 8), :] = total[:, DIM:].T[:8]
        mine[h, pl.ds(CUT + 8, CUT), :] = total[CUT:, :DIM]

    def share(i):
        for p in range(2):
            to_twin((1 - core) * half + i, p).start()

    ones = jnp.ones((TILE, DIM), BF16)
    later = lax.broadcasted_iota(jnp.int32, (TILE, TILE), 1) > lax.broadcasted_iota(
        jnp.int32, (TILE, TILE), 0
    )

    def local(h):
        total = None
        for t in range(tiles):
            at = pl.ds(t * TILE, TILE)
            f = features(qb[h, at, :])
            fq[h, at, :] = f
            sc = nt(f, fk[h, at, :])
            scores[h, at, :] = jnp.where(later, 0.0, sc).astype(BF16)
            if t < tiles - 1:
                add = tn(fk[h, at, :], jnp.concatenate([vb[h, at, :], ones], axis=1))
                total = total + add if t else add
                prior[h, t + 1] = total

    def climb(i):
        h = core * half + i
        for p in range(2):
            at = pl.ds(*CHUNKS[p])
            to_twin(h, p).wait_recv()

            @pl.when(level > 0)
            def _():
                up(i, p).wait_recv()

            below = cin[i, at]
            both = below + (mine[h, at] + theirs[h, at])

            @pl.when(level < levels - 1)
            def _():
                cout[i, at] = both
                up(i, p).start()

            @pl.when(side == 0)
            def _():
                xout[i, at] = both

            @pl.when(side == 1)
            def _():
                xout[i, at] = below

            over(i, p).start()

    def cross(i):
        for p in range(2):
            at = pl.ds(*CHUNKS[p])
            over(i, p).wait_recv()
            chip = cin[i, at] + xin[i, at]

            @pl.when(core == 0)
            def _():
                home[i, at] = chip
                pout[i, at] = chip + mine[i, at]

            @pl.when(core == 1)
            def _():
                home[i, at] = chip + theirs[i + half, at]
                pout[i, at] = chip

            prefix(i, p).start()

    def at_turn(t, step):
        @pl.when((t >= 0) & (t < half))
        def _():
            step(t)

    def steps(u):
        @pl.when(level > 0)
        def _():
            at_turn(u - 1 - 3 * level, climb)

        at_turn(u - 4 - 3 * level, cross)

    def finish(h, before):
        norm = jnp.broadcast_to(before[CUT : CUT + 1], (DIM, DIM)).T
        state = jnp.concatenate([before[:CUT], before[CUT + 8 :]], axis=0)
        start = jnp.concatenate([state, norm], axis=1)
        for t in range(tiles):
            at = pl.ds(t * TILE, TILE)
            w = (start + prior[h, t] if t else start).astype(BF16)
            a = jnp.concatenate([scores[h, at, :], fq[h, at, :]], axis=1)
            b = jnp.concatenate([vb[h, at, :], ones], axis=1)
            r = nn(a, jnp.concatenate([b, w], axis=0))
            d = r[:, DIM:]
            x = pl.reciprocal(d, approx=True)
            x = x * (2.0 - d * x)
            ob[h, at, :] = (r[:, :DIM] * x).astype(BF16)

    def close(i):
        own = core * half + i
        other = (1 - core) * half + i
        finish(own, home[i])
        store(own).start()
        for p in range(2):
            prefix(i, p).wait()
        finish(other, pin[i])
        store(other).start()

    arrive(0, half)
    fetch(2)
    state(0)
    state(half)
    near = 2 + jnp.where(level > 0, 1, 0) + jnp.where(level < levels - 1, 1, 0)
    pl.semaphore_wait(barrier, near)
    share(0)

    @pl.loop(1, half)
    def _(u):
        arrive(u, u + half)

        @pl.when(u == 1)
        def _():
            fetch(3)

        @pl.when(u > 1)
        def _():
            for j in range(half):
                load(2, q_hbm, qb, (u - 2) * half + j).start()

        state(u)
        state(u + half)
        share(u)

        @pl.when(level == 0)
        def _():
            climb(u - 1)

    @pl.when(level == 0)
    def _():
        climb(half - 1)

    tail = half + HEADS

    @pl.loop(half, tail)
    def _(u):
        load(2, q_hbm, qb, u - half).wait()
        local(u - half)
        steps(u)

    first = lax.max(tail, 6 + 3 * level)

    @pl.loop(tail, max(tail, 3 + 3 * levels) + half)
    def _(u):
        steps(u)
        at_turn(u - first, close)

    @pl.loop(0, half)
    def _(i):
        for p in range(2):
            to_twin((1 - core) * half + i, p).wait_send()

            @pl.when(level < levels - 1)
            def _():
                up(i, p).wait_send()

            over(i, p).wait_send()

    @pl.loop(0, HEADS)
    def _(h):
        store(h).wait()


def solution(mesh):
    n = mesh.shape["block"]

    def per_device(q, k, v):
        rows = q.shape[0]
        tiles = rows // TILE
        whole = pltpu.VMEM((HEADS, rows, DIM), BF16)
        totals = pltpu.VMEM((HEADS, DIM + 8, DIM), F32)
        parts = pltpu.VMEM((HEADS // 2, DIM + 8, DIM), F32)
        line = pltpu.SemaphoreType.DMA((HEADS // 2, 2))
        full = pltpu.SemaphoreType.DMA((HEADS, 2))
        return pl.pallas_call(
            functools.partial(kernel, n),
            out_shape=jax.ShapeDtypeStruct(q.shape, BF16),
            in_specs=[pl.BlockSpec(memory_space=pl.ANY)] * 3,
            out_specs=pl.BlockSpec(memory_space=pl.ANY),
            scratch_shapes=[
                whole, whole, whole, whole, whole, whole, whole,
                pltpu.VMEM((HEADS, tiles, DIM, 2 * DIM), F32),
                totals, totals, parts, parts, parts, parts, parts, parts, parts,
                pltpu.SemaphoreType.DMA((3, HEADS)),
                pltpu.SemaphoreType.DMA((HEADS,)),
                full, full,
                line, line, line, line, line, line,
            ],
            compiler_params=pltpu.CompilerParams(
                collective_id=0, has_side_effects=True, vmem_limit_bytes=50 * 2**20
            ),
        )(q, k, v)

    spec = P(("groups", "block"), None)
    return jax.shard_map(
        per_device, mesh=mesh, in_specs=(spec,) * 3, out_specs=spec, check_vma=False
    )
```

```python
import functools

import jax
import jax.numpy as jnp
from jax import lax
from jax.experimental import pallas as pl
from jax.experimental.pallas import tpu as pltpu
from jax.sharding import PartitionSpec as P

HEADS = 8
DIM = 128
TILE = 128
WIDE = 256
CUT = DIM // 2
CHUNKS = ((0, CUT + 8), (CUT + 8, CUT))
F32 = jnp.float32
BF16 = jnp.bfloat16


def features(x):
    x = x.astype(F32)
    return jnp.where(x > 0.0, x + 1.0, jnp.exp(x)).astype(BF16)


def nt(a, b):
    return lax.dot_general(a, b, (((1,), (1,)), ((), ())), preferred_element_type=F32)


def tn(a, b):
    return lax.dot_general(a, b, (((0,), (0,)), ((), ())), preferred_element_type=F32)


def nn(a, b):
    return jnp.dot(a, b, preferred_element_type=F32)


def kernel(
    n, q_hbm, k_hbm, v_hbm, o_hbm, qb, kb, vb, ob, fq, fk, scores, prior,
    mine, theirs, cin, cout, xin, xout, pin, pout, home,
    in_sem, out_sem, t_send, t_recv, z_send, z_recv, x_send, x_recv, p_send, p_recv,
):
    rows = qb.shape[1]
    tiles = rows // TILE
    half = HEADS // 2
    levels = n // 4
    me = lax.axis_index("block")
    core = lax.rem(me, 2)
    side = lax.rem(me // 2, 2)
    level = me // 4
    twin = me + 1 - 2 * core
    across = me + 2 - 4 * side

    def cols(h):
        return pl.ds(pl.multiple_of(h * DIM, DIM), DIM)

    def load(which, src, dst, h):
        return pltpu.make_async_copy(src.at[:, cols(h)], dst.at[h], in_sem.at[which, h])

    def remote(src, dst, send, recv, i, p, to):
        at = pl.ds(*CHUNKS[p])
        return pltpu.make_async_remote_copy(
            src_ref=src.at[i, at], dst_ref=dst.at[i, at], send_sem=send.at[i, p],
            recv_sem=recv.at[i, p], device_id={"block": to},
        )

    def to_twin(h, p):
        return remote(mine, theirs, t_send, t_recv, h, p, twin)

    def up(i, p):
        return remote(cout, cin, z_send, z_recv, i, p, me + 4)

    def over(i, p):
        return remote(xout, xin, x_send, x_recv, i, p, across)

    def prefix(i, p):
        return remote(pout, pin, p_send, p_recv, i, p, twin)

    def store(h):
        return pltpu.make_async_copy(ob.at[h], o_hbm.at[:, cols(h)], out_sem.at[h])

    def pair(u):
        theirs_first = (1 - core) * half + 2 * u
        return jnp.where(u < half // 2, theirs_first, core * half + 2 * u - half)

    def fetch(u):
        for h in (pair(u), pair(u) + 1):
            load(0, k_hbm, kb, h).start()
            load(1, v_hbm, vb, h).start()

    fetch(0)
    fetch(1)

    barrier = pltpu.get_barrier_semaphore()
    pl.semaphore_signal(barrier, inc=1, device_id={"block": twin})
    pl.semaphore_signal(barrier, inc=1, device_id={"block": across})

    @pl.when(level > 0)
    def _():
        pl.semaphore_signal(barrier, inc=1, device_id={"block": me - 4})

    @pl.when(level < levels - 1)
    def _():
        pl.semaphore_signal(barrier, inc=1, device_id={"block": me + 4})

    @pl.when(level == 0)
    def _():
        cin[...] = jnp.zeros(cin.shape, F32)

    def arrive(u):
        for h in (pair(u), pair(u) + 1):
            load(0, k_hbm, kb, h).wait()
            load(1, v_hbm, vb, h).wait()

    def state(h):
        ones = jnp.ones((WIDE, DIM), BF16)
        total = None
        for t in range(rows // WIDE):
            at = pl.ds(t * WIDE, WIDE)
            f = features(kb[h, at, :])
            fk[h, at, :] = f
            add = tn(f, jnp.concatenate([vb[h, at, :], ones], axis=1))
            total = total + add if t else add
        mine[h, pl.ds(0, CUT), :] = total[:CUT, :DIM]
        mine[h, pl.ds(CUT, 8), :] = total[:, DIM:].T[:8]
        mine[h, pl.ds(CUT + 8, CUT), :] = total[CUT:, :DIM]

    def share(u):
        for h in (pair(u), pair(u) + 1):
            for p in range(2):
                to_twin(h, p).start()

    ones = jnp.ones((TILE, DIM), BF16)
    later = lax.broadcasted_iota(jnp.int32, (TILE, TILE), 1) > lax.broadcasted_iota(
        jnp.int32, (TILE, TILE), 0
    )

    def local(h):
        total = None
        for t in range(tiles):
            at = pl.ds(t * TILE, TILE)
            f = features(qb[h, at, :])
            fq[h, at, :] = f
            sc = nt(f, fk[h, at, :])
            scores[h, at, :] = jnp.where(later, 0.0, sc).astype(BF16)
            if t < tiles - 1:
                add = tn(fk[h, at, :], jnp.concatenate([vb[h, at, :], ones], axis=1))
                total = total + add if t else add
                prior[h, t + 1] = total

    def climb(i):
        h = core * half + i
        for p in range(2):
            at = pl.ds(*CHUNKS[p])
            to_twin(h, p).wait_recv()

            @pl.when(level > 0)
            def _():
                up(i, p).wait_recv()

            below = cin[i, at]
            both = below + (mine[h, at] + theirs[h, at])

            @pl.when(level < levels - 1)
            def _():
                cout[i, at] = both
                up(i, p).start()

            @pl.when(side == 0)
            def _():
                xout[i, at] = both

            @pl.when(side == 1)
            def _():
                xout[i, at] = below

            over(i, p).start()

    def cross(i):
        for p in range(2):
            at = pl.ds(*CHUNKS[p])
            over(i, p).wait_recv()
            chip = cin[i, at] + xin[i, at]

            @pl.when(core == 0)
            def _():
                home[i, at] = chip
                pout[i, at] = chip + mine[i, at]

            @pl.when(core == 1)
            def _():
                home[i, at] = chip + theirs[i + half, at]
                pout[i, at] = chip

            prefix(i, p).start()

    def at_turn(t, step):
        @pl.when((t >= 0) & (t < half))
        def _():
            step(t)

    def steps(u):
        @pl.when(level > 0)
        def _():
            at_turn(u - 1 - 3 * level, climb)

        at_turn(u - 4 - 3 * level, cross)

    def finish(h, before):
        norm = jnp.broadcast_to(before[CUT : CUT + 1], (DIM, DIM)).T
        state = jnp.concatenate([before[:CUT], before[CUT + 8 :]], axis=0)
        start = jnp.concatenate([state, norm], axis=1)
        for t in range(tiles):
            at = pl.ds(t * TILE, TILE)
            w = (start + prior[h, t] if t else start).astype(BF16)
            a = jnp.concatenate([scores[h, at, :], fq[h, at, :]], axis=1)
            b = jnp.concatenate([vb[h, at, :], ones], axis=1)
            r = nn(a, jnp.concatenate([b, w], axis=0))
            d = r[:, DIM:]
            x = pl.reciprocal(d, approx=True)
            x = x * (2.0 - d * x)
            ob[h, at, :] = (r[:, :DIM] * x).astype(BF16)

    def close(i):
        own = core * half + i
        other = (1 - core) * half + i
        finish(own, home[i])
        store(own).start()
        for p in range(2):
            prefix(i, p).wait()
        finish(other, pin[i])
        store(other).start()

    arrive(0)
    fetch(2)
    state(pair(0))
    state(pair(0) + 1)
    near = 2 + jnp.where(level > 0, 1, 0) + jnp.where(level < levels - 1, 1, 0)
    pl.semaphore_wait(barrier, near)
    share(0)

    @pl.loop(1, half)
    def _(u):
        arrive(u)

        @pl.when(u == 1)
        def _():
            fetch(3)

        @pl.when(u > 1)
        def _():
            for j in range(half):
                load(2, q_hbm, qb, (u - 2) * half + j).start()

        state(pair(u))
        state(pair(u) + 1)

        @pl.when(u < half // 2)
        def _():
            share(u)

        @pl.when((level == 0) & (u >= half // 2))
        def _():
            climb(2 * u - half)
            climb(2 * u - half + 1)

    tail = half + HEADS

    @pl.loop(half, tail)
    def _(u):
        load(2, q_hbm, qb, u - half).wait()
        local(u - half)
        steps(u)

    first = lax.max(tail, 6 + 3 * level)

    @pl.loop(tail, max(tail, 3 + 3 * levels) + half)
    def _(u):
        steps(u)
        at_turn(u - first, close)

    @pl.loop(0, half)
    def _(i):
        for p in range(2):
            to_twin((1 - core) * half + i, p).wait_send()

            @pl.when(level < levels - 1)
            def _():
                up(i, p).wait_send()

            over(i, p).wait_send()

    @pl.loop(0, HEADS)
    def _(h):
        store(h).wait()


def solution(mesh):
    n = mesh.shape["block"]

    def per_device(q, k, v):
        rows = q.shape[0]
        tiles = rows // TILE
        whole = pltpu.VMEM((HEADS, rows, DIM), BF16)
        totals = pltpu.VMEM((HEADS, DIM + 8, DIM), F32)
        parts = pltpu.VMEM((HEADS // 2, DIM + 8, DIM), F32)
        line = pltpu.SemaphoreType.DMA((HEADS // 2, 2))
        full = pltpu.SemaphoreType.DMA((HEADS, 2))
        return pl.pallas_call(
            functools.partial(kernel, n),
            out_shape=jax.ShapeDtypeStruct(q.shape, BF16),
            in_specs=[pl.BlockSpec(memory_space=pl.ANY)] * 3,
            out_specs=pl.BlockSpec(memory_space=pl.ANY),
            scratch_shapes=[
                whole, whole, whole, whole, whole, whole, whole,
                pltpu.VMEM((HEADS, tiles, DIM, 2 * DIM), F32),
                totals, totals, parts, parts, parts, parts, parts, parts, parts,
                pltpu.SemaphoreType.DMA((3, HEADS)),
                pltpu.SemaphoreType.DMA((HEADS,)),
                full, full,
                line, line, line, line, line, line,
            ],
            compiler_params=pltpu.CompilerParams(
                collective_id=0, has_side_effects=True, vmem_limit_bytes=50 * 2**20
            ),
        )(q, k, v)

    spec = P(("groups", "block"), None)
    return jax.shard_map(
        per_device, mesh=mesh, in_specs=(spec,) * 3, out_specs=spec, check_vma=False
    )
```

```python
import functools

import jax
import jax.numpy as jnp
from jax import lax
from jax.experimental import pallas as pl
from jax.experimental.pallas import tpu as pltpu
from jax.sharding import PartitionSpec as P

HEADS = 8
DIM = 128
TILE = 128
WIDE = 256
CUT = DIM // 2
CHUNKS = ((0, CUT + 8), (CUT + 8, CUT))
F32 = jnp.float32
BF16 = jnp.bfloat16


def features(x):
    x = x.astype(F32)
    return jnp.where(x > 0.0, x + 1.0, jnp.exp(x)).astype(BF16)


def nt(a, b):
    return lax.dot_general(a, b, (((1,), (1,)), ((), ())), preferred_element_type=F32)


def tn(a, b):
    return lax.dot_general(a, b, (((0,), (0,)), ((), ())), preferred_element_type=F32)


def nn(a, b):
    return jnp.dot(a, b, preferred_element_type=F32)


def kernel(
    n, q_hbm, k_hbm, v_hbm, o_hbm, qb, kb, vb, ob, fq, fk, scores, prior,
    mine, theirs, cin, cout, xin, xout, pin, pout, home,
    in_sem, out_sem, t_send, t_recv, z_send, z_recv, x_send, x_recv, p_send, p_recv,
):
    rows = qb.shape[1]
    tiles = rows // TILE
    half = HEADS // 2
    levels = n // 4
    me = lax.axis_index("block")
    core = lax.rem(me, 2)
    side = lax.rem(me // 2, 2)
    level = me // 4
    twin = me + 1 - 2 * core
    across = me + 2 - 4 * side

    def cols(h):
        return pl.ds(pl.multiple_of(h * DIM, DIM), DIM)

    def load(which, src, dst, h):
        return pltpu.make_async_copy(src.at[:, cols(h)], dst.at[h], in_sem.at[which, h])

    def remote(src, dst, send, recv, i, p, to):
        at = pl.ds(*CHUNKS[p])
        return pltpu.make_async_remote_copy(
            src_ref=src.at[i, at], dst_ref=dst.at[i, at], send_sem=send.at[i, p],
            recv_sem=recv.at[i, p], device_id={"block": to},
        )

    def to_twin(h, p):
        return remote(mine, theirs, t_send, t_recv, h, p, twin)

    def up(i, p):
        return remote(cout, cin, z_send, z_recv, i, p, me + 4)

    def over(i, p):
        return remote(xout, xin, x_send, x_recv, i, p, across)

    def prefix(i, p):
        return remote(pout, pin, p_send, p_recv, i, p, twin)

    def store(h):
        return pltpu.make_async_copy(ob.at[h], o_hbm.at[:, cols(h)], out_sem.at[h])

    def pair(u):
        theirs_first = (1 - core) * half + 2 * u
        return jnp.where(u < half // 2, theirs_first, core * half + 2 * u - half)

    def fetch(u):
        for h in (pair(u), pair(u) + 1):
            load(0, k_hbm, kb, h).start()
            load(1, v_hbm, vb, h).start()

    fetch(0)
    fetch(1)

    barrier = pltpu.get_barrier_semaphore()
    pl.semaphore_signal(barrier, inc=1, device_id={"block": twin})
    pl.semaphore_signal(barrier, inc=1, device_id={"block": across})

    @pl.when(level > 0)
    def _():
        pl.semaphore_signal(barrier, inc=1, device_id={"block": me - 4})

    @pl.when(level < levels - 1)
    def _():
        pl.semaphore_signal(barrier, inc=1, device_id={"block": me + 4})

    @pl.when(level == 0)
    def _():
        cin[...] = jnp.zeros(cin.shape, F32)

    def arrive(u):
        for h in (pair(u), pair(u) + 1):
            load(0, k_hbm, kb, h).wait()
            load(1, v_hbm, vb, h).wait()

    def state(h):
        ones = jnp.ones((WIDE, DIM), BF16)
        total = None
        for t in range(rows // WIDE):
            at = pl.ds(t * WIDE, WIDE)
            f = features(kb[h, at, :])
            fk[h, at, :] = f
            add = tn(f, jnp.concatenate([vb[h, at, :], ones], axis=1))
            total = total + add if t else add
        mine[h, pl.ds(0, CUT), :] = total[:CUT, :DIM]
        mine[h, pl.ds(CUT, 8), :] = total[:, DIM:].T[:8]
        mine[h, pl.ds(CUT + 8, CUT), :] = total[CUT:, :DIM]

    def share(u):
        for h in (pair(u), pair(u) + 1):
            for p in range(2):
                to_twin(h, p).start()

    ones = jnp.ones((TILE, DIM), BF16)
    later = lax.broadcasted_iota(jnp.int32, (TILE, TILE), 1) > lax.broadcasted_iota(
        jnp.int32, (TILE, TILE), 0
    )

    def local(h):
        total = None
        for t in range(tiles):
            at = pl.ds(t * TILE, TILE)
            f = features(qb[h, at, :])
            fq[h, at, :] = f
            sc = nt(f, fk[h, at, :])
            scores[h, at, :] = jnp.where(later, 0.0, sc).astype(BF16)
            if t < tiles - 1:
                add = tn(fk[h, at, :], jnp.concatenate([vb[h, at, :], ones], axis=1))
                total = total + add if t else add
                prior[h, t + 1] = total

    def climb(i):
        h = core * half + i
        for p in range(2):
            at = pl.ds(*CHUNKS[p])
            to_twin(h, p).wait_recv()

            @pl.when(level > 0)
            def _():
                up(i, p).wait_recv()

            below = cin[i, at]
            both = below + (mine[h, at] + theirs[h, at])

            @pl.when(level < levels - 1)
            def _():
                cout[i, at] = both
                up(i, p).start()

            @pl.when(side == 0)
            def _():
                xout[i, at] = both

            @pl.when(side == 1)
            def _():
                xout[i, at] = below

            over(i, p).start()

    def cross(i):
        for p in range(2):
            at = pl.ds(*CHUNKS[p])
            over(i, p).wait_recv()
            chip = cin[i, at] + xin[i, at]

            @pl.when(core == 0)
            def _():
                home[i, at] = chip
                pout[i, at] = chip + mine[i, at]

            @pl.when(core == 1)
            def _():
                home[i, at] = chip + theirs[i + half, at]
                pout[i, at] = chip

            prefix(i, p).start()

    def at_turn(t, step):
        @pl.when((t >= 0) & (t < half))
        def _():
            step(t)

    def steps(u):
        @pl.when(level > 0)
        def _():
            at_turn(u - 1 - 3 * level, climb)

        at_turn(u - 4 - 3 * level, cross)

    def finish(h, before):
        norm = jnp.broadcast_to(before[CUT : CUT + 1], (DIM, DIM)).T
        state = jnp.concatenate([before[:CUT], before[CUT + 8 :]], axis=0)
        start = jnp.concatenate([state, norm], axis=1)
        for t in range(tiles):
            at = pl.ds(t * TILE, TILE)
            w = (start + prior[h, t] if t else start).astype(BF16)
            a = jnp.concatenate([scores[h, at, :], fq[h, at, :]], axis=1)
            b = jnp.concatenate([vb[h, at, :], ones], axis=1)
            r = nn(a, jnp.concatenate([b, w], axis=0))
            d = r[:, DIM:]
            x = pl.reciprocal(d, approx=True)
            x = x * (2.0 - d * x)
            ob[h, at, :] = (r[:, :DIM] * x).astype(BF16)

    def close_own(i):
        own = core * half + i
        finish(own, home[i])
        store(own).start()

    def close_other(i):
        other = (1 - core) * half + i
        for p in range(2):
            prefix(i, p).wait()
        finish(other, pin[i])
        store(other).start()

    arrive(0)
    fetch(2)
    state(pair(0))
    state(pair(0) + 1)
    near = 2 + jnp.where(level > 0, 1, 0) + jnp.where(level < levels - 1, 1, 0)
    pl.semaphore_wait(barrier, near)
    share(0)

    @pl.loop(1, half)
    def _(u):
        arrive(u)

        @pl.when(u == 1)
        def _():
            fetch(3)

        @pl.when(u > 1)
        def _():
            for j in range(half):
                load(2, q_hbm, qb, (u - 2) * half + j).start()

        state(pair(u))
        state(pair(u) + 1)

        @pl.when(u < half // 2)
        def _():
            share(u)

        @pl.when((level == 0) & (u >= half // 2))
        def _():
            climb(2 * u - half)
            climb(2 * u - half + 1)

    tail = half + HEADS

    @pl.loop(half, tail)
    def _(u):
        load(2, q_hbm, qb, u - half).wait()
        local(u - half)
        steps(u)

    first = lax.max(tail, 4 + 3 * level)

    @pl.loop(tail, max(tail, 1 + 3 * levels) + half + 1)
    def _(u):
        steps(u)
        at_turn(u - first - 1, close_other)
        at_turn(u - first, close_own)

    @pl.loop(0, half)
    def _(i):
        for p in range(2):
            to_twin((1 - core) * half + i, p).wait_send()

            @pl.when(level < levels - 1)
            def _():
                up(i, p).wait_send()

            over(i, p).wait_send()

    @pl.loop(0, HEADS)
    def _(h):
        store(h).wait()


def solution(mesh):
    n = mesh.shape["block"]

    def per_device(q, k, v):
        rows = q.shape[0]
        tiles = rows // TILE
        whole = pltpu.VMEM((HEADS, rows, DIM), BF16)
        totals = pltpu.VMEM((HEADS, DIM + 8, DIM), F32)
        parts = pltpu.VMEM((HEADS // 2, DIM + 8, DIM), F32)
        line = pltpu.SemaphoreType.DMA((HEADS // 2, 2))
        full = pltpu.SemaphoreType.DMA((HEADS, 2))
        return pl.pallas_call(
            functools.partial(kernel, n),
            out_shape=jax.ShapeDtypeStruct(q.shape, BF16),
            in_specs=[pl.BlockSpec(memory_space=pl.ANY)] * 3,
            out_specs=pl.BlockSpec(memory_space=pl.ANY),
            scratch_shapes=[
                whole, whole, whole, whole, whole, whole, whole,
                pltpu.VMEM((HEADS, tiles, DIM, 2 * DIM), F32),
                totals, totals, parts, parts, parts, parts, parts, parts, parts,
                pltpu.SemaphoreType.DMA((3, HEADS)),
                pltpu.SemaphoreType.DMA((HEADS,)),
                full, full,
                line, line, line, line, line, line,
            ],
            compiler_params=pltpu.CompilerParams(
                collective_id=0, has_side_effects=True, vmem_limit_bytes=50 * 2**20
            ),
        )(q, k, v)

    spec = P(("groups", "block"), None)
    return jax.shard_map(
        per_device, mesh=mesh, in_specs=(spec,) * 3, out_specs=spec, check_vma=False
    )
```

```python
import functools

import jax
import jax.numpy as jnp
from jax import lax
from jax.experimental import pallas as pl
from jax.experimental.pallas import tpu as pltpu
from jax.sharding import PartitionSpec as P

HEADS = 8
DIM = 128
TILE = 128
WIDE = 256
CUT = DIM // 2
CHUNKS = ((0, CUT + 8), (CUT + 8, CUT))
F32 = jnp.float32
BF16 = jnp.bfloat16


def features(x):
    x = x.astype(F32)
    return jnp.where(x > 0.0, x + 1.0, jnp.exp(x)).astype(BF16)


def nt(a, b):
    return lax.dot_general(a, b, (((1,), (1,)), ((), ())), preferred_element_type=F32)


def tn(a, b):
    return lax.dot_general(a, b, (((0,), (0,)), ((), ())), preferred_element_type=F32)


def nn(a, b):
    return jnp.dot(a, b, preferred_element_type=F32)


def kernel(
    n, q_hbm, k_hbm, v_hbm, o_hbm, qb, kb, vb, ob, fq, fk, scores, prior,
    mine, theirs, cin, cout, xin, xout, pin, pout, home,
    in_sem, out_sem, t_send, t_recv, z_send, z_recv, x_send, x_recv, p_send, p_recv,
):
    rows = qb.shape[1]
    tiles = rows // TILE
    half = HEADS // 2
    levels = n // 4
    me = lax.axis_index("block")
    core = lax.rem(me, 2)
    side = lax.rem(me // 2, 2)
    level = me // 4
    twin = me + 1 - 2 * core
    across = me + 2 - 4 * side

    def cols(h):
        return pl.ds(pl.multiple_of(h * DIM, DIM), DIM)

    def load(which, src, dst, h):
        return pltpu.make_async_copy(src.at[:, cols(h)], dst.at[h], in_sem.at[which, h])

    def remote(src, dst, send, recv, i, p, to):
        at = pl.ds(*CHUNKS[p])
        return pltpu.make_async_remote_copy(
            src_ref=src.at[i, at], dst_ref=dst.at[i, at], send_sem=send.at[i, p],
            recv_sem=recv.at[i, p], device_id={"block": to},
        )

    def to_twin(h, p):
        return remote(mine, theirs, t_send, t_recv, h, p, twin)

    def up(i, p):
        return remote(cout, cin, z_send, z_recv, i, p, me + 4)

    def over(i, p):
        return remote(xout, xin, x_send, x_recv, i, p, across)

    def prefix(i, p):
        return remote(pout, pin, p_send, p_recv, i, p, twin)

    def store(h):
        return pltpu.make_async_copy(ob.at[h], o_hbm.at[:, cols(h)], out_sem.at[h])

    def pair(u):
        theirs_first = (1 - core) * half + 2 * u
        return jnp.where(u < half // 2, theirs_first, core * half + 2 * u - half)

    def fetch(u):
        for h in (pair(u), pair(u) + 1):
            load(0, k_hbm, kb, h).start()
            load(1, v_hbm, vb, h).start()

    fetch(0)
    fetch(1)

    barrier = pltpu.get_barrier_semaphore()
    pl.semaphore_signal(barrier, inc=1, device_id={"block": twin})
    pl.semaphore_signal(barrier, inc=1, device_id={"block": across})

    @pl.when(level > 0)
    def _():
        pl.semaphore_signal(barrier, inc=1, device_id={"block": me - 4})

    @pl.when(level < levels - 1)
    def _():
        pl.semaphore_signal(barrier, inc=1, device_id={"block": me + 4})

    @pl.when(level == 0)
    def _():
        cin[...] = jnp.zeros(cin.shape, F32)

    def arrive(u):
        for h in (pair(u), pair(u) + 1):
            load(0, k_hbm, kb, h).wait()
            load(1, v_hbm, vb, h).wait()

    def state(h):
        ones = jnp.ones((WIDE, DIM), BF16)
        total = None
        for t in range(rows // WIDE):
            at = pl.ds(t * WIDE, WIDE)
            f = features(kb[h, at, :])
            fk[h, at, :] = f
            add = tn(f, jnp.concatenate([vb[h, at, :], ones], axis=1))
            total = total + add if t else add
        mine[h, pl.ds(0, CUT), :] = total[:CUT, :DIM]
        mine[h, pl.ds(CUT, 8), :] = total[:, DIM:].T[:8]
        mine[h, pl.ds(CUT + 8, CUT), :] = total[CUT:, :DIM]

    def share(u):
        for h in (pair(u), pair(u) + 1):
            for p in range(2):
                to_twin(h, p).start()

    ones = jnp.ones((TILE, DIM), BF16)
    later = lax.broadcasted_iota(jnp.int32, (TILE, TILE), 1) > lax.broadcasted_iota(
        jnp.int32, (TILE, TILE), 0
    )

    def local(h):
        total = None
        for t in range(tiles):
            at = pl.ds(t * TILE, TILE)
            f = features(qb[h, at, :])
            fq[h, at, :] = f
            sc = nt(f, fk[h, at, :])
            scores[h, at, :] = jnp.where(later, 0.0, sc).astype(BF16)
            if t < tiles - 1:
                add = tn(fk[h, at, :], jnp.concatenate([vb[h, at, :], ones], axis=1))
                total = total + add if t else add
                prior[h, t + 1] = total

    def climb(i):
        h = core * half + i
        for p in range(2):
            at = pl.ds(*CHUNKS[p])
            to_twin(h, p).wait_recv()

            @pl.when(level > 0)
            def _():
                up(i, p).wait_recv()

            below = cin[i, at]
            both = below + (mine[h, at] + theirs[h, at])

            @pl.when(level < levels - 1)
            def _():
                cout[i, at] = both
                up(i, p).start()

            @pl.when(side == 0)
            def _():
                xout[i, at] = both

            @pl.when(side == 1)
            def _():
                xout[i, at] = below

            over(i, p).start()

    def cross(i):
        for p in range(2):
            at = pl.ds(*CHUNKS[p])
            over(i, p).wait_recv()
            chip = cin[i, at] + xin[i, at]

            @pl.when(core == 0)
            def _():
                home[i, at] = chip
                pout[i, at] = chip + mine[i, at]

            @pl.when(core == 1)
            def _():
                home[i, at] = chip + theirs[i + half, at]
                pout[i, at] = chip

            prefix(i, p).start()

    def at_turn(t, step):
        @pl.when((t >= 0) & (t < half))
        def _():
            step(t)

    def steps(u):
        @pl.when(level > 0)
        def _():
            at_turn(u - 1 - 3 * level, climb)

        at_turn(u - lax.max(half, 3 + 3 * level), cross)

    def finish(h, before):
        norm = jnp.broadcast_to(before[CUT : CUT + 1], (DIM, DIM)).T
        state = jnp.concatenate([before[:CUT], before[CUT + 8 :]], axis=0)
        start = jnp.concatenate([state, norm], axis=1)
        for t in range(tiles):
            at = pl.ds(t * TILE, TILE)
            w = (start + prior[h, t] if t else start).astype(BF16)
            a = jnp.concatenate([scores[h, at, :], fq[h, at, :]], axis=1)
            b = jnp.concatenate([vb[h, at, :], ones], axis=1)
            r = nn(a, jnp.concatenate([b, w], axis=0))
            d = r[:, DIM:]
            x = pl.reciprocal(d, approx=True)
            x = x * (2.0 - d * x)
            ob[h, at, :] = (r[:, :DIM] * x).astype(BF16)

    def close_own(i):
        own = core * half + i
        finish(own, home[i])
        store(own).start()

    def close_other(i):
        other = (1 - core) * half + i
        for p in range(2):
            prefix(i, p).wait()
        finish(other, pin[i])
        store(other).start()

    arrive(0)
    fetch(2)
    state(pair(0))
    state(pair(0) + 1)
    near = 2 + jnp.where(level > 0, 1, 0) + jnp.where(level < levels - 1, 1, 0)
    pl.semaphore_wait(barrier, near)
    share(0)

    @pl.loop(1, half)
    def _(u):
        arrive(u)

        @pl.when(u == 1)
        def _():
            fetch(3)

        @pl.when(u > 1)
        def _():
            for j in range(half):
                load(2, q_hbm, qb, (u - 2) * half + j).start()

        state(pair(u))
        state(pair(u) + 1)

        @pl.when(u < half // 2)
        def _():
            share(u)

        @pl.when((level == 0) & (u >= half // 2))
        def _():
            climb(2 * u - half)
            climb(2 * u - half + 1)

    tail = half + HEADS

    @pl.loop(half, tail)
    def _(u):
        load(2, q_hbm, qb, u - half).wait()
        local(u - half)
        steps(u)

    first = lax.max(tail, 3 + 3 * level)

    @pl.loop(tail, max(tail, 3 * levels) + half + 1)
    def _(u):
        steps(u)
        at_turn(u - first - 1, close_other)
        at_turn(u - first, close_own)

    @pl.loop(0, half)
    def _(i):
        for p in range(2):
            to_twin((1 - core) * half + i, p).wait_send()

            @pl.when(level < levels - 1)
            def _():
                up(i, p).wait_send()

            over(i, p).wait_send()

    @pl.loop(0, HEADS)
    def _(h):
        store(h).wait()


def solution(mesh):
    n = mesh.shape["block"]

    def per_device(q, k, v):
        rows = q.shape[0]
        tiles = rows // TILE
        whole = pltpu.VMEM((HEADS, rows, DIM), BF16)
        totals = pltpu.VMEM((HEADS, DIM + 8, DIM), F32)
        parts = pltpu.VMEM((HEADS // 2, DIM + 8, DIM), F32)
        line = pltpu.SemaphoreType.DMA((HEADS // 2, 2))
        full = pltpu.SemaphoreType.DMA((HEADS, 2))
        return pl.pallas_call(
            functools.partial(kernel, n),
            out_shape=jax.ShapeDtypeStruct(q.shape, BF16),
            in_specs=[pl.BlockSpec(memory_space=pl.ANY)] * 3,
            out_specs=pl.BlockSpec(memory_space=pl.ANY),
            scratch_shapes=[
                whole, whole, whole, whole, whole, whole, whole,
                pltpu.VMEM((HEADS, tiles, DIM, 2 * DIM), F32),
                totals, totals, parts, parts, parts, parts, parts, parts, parts,
                pltpu.SemaphoreType.DMA((3, HEADS)),
                pltpu.SemaphoreType.DMA((HEADS,)),
                full, full,
                line, line, line, line, line, line,
            ],
            compiler_params=pltpu.CompilerParams(
                collective_id=0, has_side_effects=True, vmem_limit_bytes=50 * 2**20
            ),
        )(q, k, v)

    spec = P(("groups", "block"), None)
    return jax.shard_map(
        per_device, mesh=mesh, in_specs=(spec,) * 3, out_specs=spec, check_vma=False
    )
```
